32 devices in a mesh: chain: 2 (over y), dp: 8 (over z, x), rep: 2 (over core).
Axes of the slice: x: 2, y: 2, z: 4, core: 2. Of those that a mesh axis runs over, the one named last changes fastest.
Arguments:
- descriptors: float32 [2, 32, 128, 256], P(None, ('dp', 'rep')), may hold values from -6 to 6
- counts: int32 [2, 32], P(None, ('dp', 'rep')), may hold values from 0 to 128, as said below
- struct_ids: int32 [2, 32, 128], P(None, ('dp', 'rep')), may hold values from 0 to 31
- ref_energy: float32 [512], P(('dp', 'rep')), may hold values from -9 to 9
- first_layer: float32 [4, 131072], P('chain', ('dp', 'rep')), parts along dimension 0, may hold values from -0.375 to 0.375
- second_layer: float32 [4, 262144], P('chain', ('dp', 'rep')), parts along dimension 0, may hold values from -0.25 to 0.25
- vectors: float32 [4, 3, 512], P('chain'), parts along dimension 0, may hold values from -0.6 to 0.6
- first_momentum: float32 [4, 131072], P('chain', ('dp', 'rep')), parts along dimension 0, may hold values from -6 to 6
- second_momentum: float32 [4, 262144], P('chain', ('dp', 'rep')), parts along dimension 0, may hold values from -6 to 6
- vector_momentum: float32 [4, 3, 512], P('chain'), parts along dimension 0, may hold values from -6 to 6
Outputs:
- new_first: float32 [4, 131072], P('chain', ('dp', 'rep')), parts along dimension 0
- new_second: float32 [4, 262144], P('chain', ('dp', 'rep')), parts along dimension 0
- new_vectors: float32 [4, 3, 512], P('chain'), parts along dimension 0
- new_first_mom: float32 [4, 131072], P('chain', ('dp', 'rep')), parts along dimension 0
- new_second_mom: float32 [4, 262144], P('chain', ('dp', 'rep')), parts along dimension 0
- new_vector_mom: float32 [4, 3, 512], P('chain'), parts along dimension 0
- potential: float32 [2], P('chain'), parts along dimension 0
- force_partials: float32 [4, 32, 128, 256], P('chain', ('dp', 'rep')), parts along dimension 0
The draws below stay inside these ranges and needn't reach their ends.
There are 2 independent parts, one for each index of `chain`. The reference program is written for one: setup_inputs(seed, part) draws one part's arguments, and reference() takes and returns one part's arrays. A program takes and returns all parts, laid end to end along the dimension named above; an argument that names none is the same for every part. Nothing has to cross between parts.
Inputs may be any that keep to these rules, and one draw needn't show every extreme that they name: `counts`: in each element, the 2 block slots of one device hold their blocks with atoms first; each such block but the last holds 128 atoms, the later slots hold 0. For each element and each device d below 8 along dp+rep, devices d and d + 8 hold at most 2 blocks with atoms together, and this is reached by some pair in every draw.
All inputs are finite; a program needn't handle non-finite values.
Results may differ from the reference program's by a relative error of at most 0.0003.
Values sent between devices are 32-bit elements; how exact they have to be, the bound alone decides.
No kernel may reach another device: no remote copies, remote signals or barrier semaphores. Data moves between devices by JAX's collectives and lax.ppermute only.
A program may use at most 192 MiB of HBM per device.

```python
import jax
import jax.numpy as jnp
from jax import lax

D = 256
H = 512
ATOMS = 128
ELEM = 2
SLOTS = 2
STRUCT_DEV = 32
SHARDS = 16
HALF = 8
BLOCKS = 32
STRUCTS = 512


def draw_counts(key, part):
    key = jax.random.fold_in(key, 11)
    keys = jax.random.split(key, 5)
    total = jax.random.randint(keys[0], (ELEM, HALF), 0, SLOTS + 1)
    spread = jax.random.randint(keys[1], (ELEM, HALF), 0, SLOTS + 1)
    lower = spread % (total + 1)
    chosen = jax.random.randint(keys[2], (), 0, HALF)
    side = jax.random.randint(keys[3], (), 0, 2)
    pinned = jnp.arange(HALF)[None, :] == chosen
    total = jnp.where(pinned, SLOTS, total)
    lower = jnp.where(pinned, SLOTS * (1 - side), lower)
    used = jnp.concatenate([lower, total - lower], axis=1)
    last = jax.random.randint(keys[4], (ELEM, SHARDS), 1, ATOMS + 1)
    slot = jnp.arange(SLOTS)[None, None, :]
    before = used[:, :, None] - 1
    filled = jnp.where(slot < before, ATOMS, jnp.where(slot == before, last[:, :, None], 0))
    return filled.reshape(ELEM, SHARDS * SLOTS).astype(jnp.int32)


def draw_ref_energy(key, part):
    key = jax.random.fold_in(key, 23)
    place = jnp.arange(STRUCTS, dtype=jnp.float32) / max(STRUCTS - 1, 1)
    base = jnp.clip(jax.random.normal(key, (STRUCTS,), jnp.float32), -3.0, 3.0)
    return (base * (1.0 + 2.0 * place)).astype(jnp.float32)


def place_ends(entries, stream_key, smallest, largest):
    shape = entries.shape
    spot = [jax.random.randint(jax.random.fold_in(stream_key, axis), (), 0, shape[axis]) for axis in range(len(shape))]
    entries = entries.at[tuple(spot)].set(smallest)
    longest = shape.index(max(shape))
    spot[longest] = (spot[longest] + 1) % shape[longest]
    return entries.at[tuple(spot)].set(largest)


def raised(drawn, stream_key, source, target, parts, factor):
    owner, partner = [(jnp.arange(drawn.shape[axis_at]) // (drawn.shape[axis_at] // parts)).reshape([-1 if axis == axis_at else 1 for axis in range(drawn.ndim)]) for axis_at in (source, target)]
    chosen = jax.random.permutation(stream_key, parts)[partner]
    strong = (owner == chosen) | (owner == (partner + parts // 2) % parts)
    return jnp.where(strong, factor * drawn, drawn)


def shard_levels(rng, extent, pieces, least, high):
    level, own = 1.0, jax.random.fold_in(rng, 6)
    for axis_at, blocks in pieces:
        heights = jnp.exp(jax.random.uniform(jax.random.fold_in(own, axis_at), (blocks,), jnp.float32, least / len(pieces), high / len(pieces)))
        level = level * jnp.repeat(heights, extent[axis_at] // blocks).reshape([-1 if axis == axis_at else 1 for axis in range(len(extent))])
    return level


def gaussian(own_key, shape, deviation, most, shards=(), kind=jnp.bfloat16):
    entries = jax.random.normal(own_key, shape, jnp.float32) * deviation
    if len(shards) > 0:
        entries = shard_levels(own_key, shape, shards, -0.22, 0.18) * entries
    return jnp.clip(entries, min=-most, max=most).astype(kind)


def noise_with(key, dims, deviation, reach, pieces, heavy, held_as=jnp.bfloat16):
    entries = deviation * jax.random.normal(key, dims, jnp.float32)
    if pieces:
        entries = entries * shard_levels(key, dims, pieces, -0.22, 0.18)
    return jnp.clip(raised(entries, jax.random.fold_in(key, 3), *heavy), -reach, reach).astype(held_as)


def setup_inputs(seed: int = 0, part: int = 0) -> dict:
    seeds = jax.random.split(jax.random.key(seed), 11)
    part_splits = jax.random.split(jax.random.fold_in(seeds[10], part), 11)
    return {
        "descriptors": noise_with(seeds[0], (ELEM, BLOCKS, ATOMS, D), 1.0, 6.0, ((1, 16),), (1, 3, 16, 2.0), jnp.float32),
        "counts": draw_counts(jax.random.fold_in(seeds[10], 71), part),
        "struct_ids": place_ends(jax.random.randint(seeds[2], (ELEM, BLOCKS, ATOMS), 0, STRUCT_DEV), jax.random.fold_in(seeds[2], 1), 0, STRUCT_DEV - 1).astype(jnp.int32),
        "ref_energy": draw_ref_energy(jax.random.fold_in(seeds[10], 71), part),
        "first_layer": gaussian(part_splits[4], (ELEM, D * H), D ** -0.5, 0.375, ((1, 16),), jnp.float32),
        "second_layer": gaussian(part_splits[5], (ELEM, H * H), H ** -0.5, 0.25, ((1, 16),), jnp.float32),
        "vectors": gaussian(part_splits[6], (ELEM, 3, H), 0.1, 0.6, (), jnp.float32),
        "first_momentum": gaussian(part_splits[7], (ELEM, D * H), 1.0, 6.0, ((1, 16),), jnp.float32),
        "second_momentum": gaussian(part_splits[8], (ELEM, H * H), 1.0, 6.0, ((1, 16),), jnp.float32),
        "vector_momentum": gaussian(part_splits[9], (ELEM, 3, H), 1.0, 6.0, (), jnp.float32),
    }


NOISE_VAR = 0.1
STEP_SIZE = 0.01
HIGH = lax.Precision.HIGHEST

def element_energies(first, second, vectors, desc):
    lower = jnp.einsum('erf,efj->erj', desc, first, precision=HIGH) + vectors[:, 0][:, None, :]
    hidden = jnp.tanh(lower)
    upper = jnp.einsum('erj,ejk->erk', hidden, second, precision=HIGH) + vectors[:, 1][:, None, :]
    top = jnp.tanh(upper)
    return jnp.einsum('erk,ek->er', top, vectors[:, 2], precision=HIGH)

def shard_terms(params, desc, counts, ids, refs):
    nelem, slots, atoms, width = desc.shape
    live = (jnp.arange(atoms, dtype=jnp.int32)[None, None, :] < counts[:, :, None]).astype(jnp.float32)
    member = (ids[..., None] == jnp.arange(refs.shape[0], dtype=jnp.int32)[None, None, None, :]).astype(jnp.float32)

    def potential_of(weights, block):
        raw = element_energies(weights[0], weights[1], weights[2], block.reshape(nelem, slots * atoms, width))
        energies = raw.reshape(nelem, slots, atoms) * live
        total = jnp.einsum('ebas,eba->s', member, energies, precision=HIGH)
        count = jnp.einsum('ebas,eba->s', member, live, precision=HIGH)
        error = total / jnp.maximum(count, 1.0) - refs
        return jnp.sum(error * error) / (2.0 * NOISE_VAR)
    value, pull = jax.vjp(potential_of, params, desc)
    grads, partials = pull(jnp.ones_like(value))
    return (value, grads, partials)

def reference(descriptors, counts, struct_ids, ref_energy, first_layer, second_layer, vectors, first_momentum, second_momentum, vector_momentum):
    nelem = descriptors.shape[0]
    params = (first_layer.reshape(nelem, D, H), second_layer.reshape(nelem, H, H), vectors)
    desc = descriptors.reshape(nelem, SHARDS, SLOTS, ATOMS, D).transpose(1, 0, 2, 3, 4)
    counts_by = counts.reshape(nelem, SHARDS, SLOTS).transpose(1, 0, 2)
    ids_by = struct_ids.reshape(nelem, SHARDS, SLOTS, ATOMS).transpose(1, 0, 2, 3)
    refs_by = ref_energy.reshape(SHARDS, STRUCT_DEV)

    def visit(carry, item):
        grads, total = carry
        value, piece, partials = shard_terms(params, item[0], item[1], item[2], item[3])
        grads = jax.tree.map(lambda left, right: left + right, grads, piece)
        return ((grads, total + value), partials)
    start = (jax.tree.map(jnp.zeros_like, params), jnp.zeros((), jnp.float32))
    (grads, potential_sum), stacked = lax.scan(visit, start, (desc, counts_by, ids_by, refs_by))
    force_partials = stacked.transpose(1, 0, 2, 3, 4).reshape(descriptors.shape)
    new_first_mom = first_momentum - STEP_SIZE * grads[0].reshape(first_momentum.shape)
    new_second_mom = second_momentum - STEP_SIZE * grads[1].reshape(second_momentum.shape)
    new_vector_mom = vector_momentum - STEP_SIZE * grads[2]
    new_first = first_layer + STEP_SIZE * new_first_mom
    new_second = second_layer + STEP_SIZE * new_second_mom
    new_vectors = vectors + STEP_SIZE * new_vector_mom
    potential = (potential_sum / STRUCTS).reshape(1)
    return (new_first, new_second, new_vectors, new_first_mom, new_second_mom, new_vector_mom, potential, force_partials)
```

```python
import jax
import jax.numpy as jnp
from jax import lax
from jax.experimental import pallas as pl
from jax.experimental.pallas import tpu as pltpu
from jax.sharding import PartitionSpec as P

NOISE_VAR = 0.1
STEP_SIZE = 0.01
HIGH = lax.Precision.HIGHEST
F32 = jnp.float32
BF16 = jnp.bfloat16
VMEM = pltpu.VMEM
LIMIT = 32 * 1024 * 1024

NT = (((1,), (1,)), ((), ()))
TN = (((0,), (0,)), ((), ()))
NN = (((1,), (0,)), ((), ()))


def split(x):
    high = x.astype(BF16)
    return high, (x - high.astype(F32)).astype(BF16)


def product(left, right, dims):
    one = lambda a, b: lax.dot_general(a, b, dims, preferred_element_type=F32)
    return one(left[0], right[0]) + (one(left[0], right[1]) + one(left[1], right[0]))


def call(kernel, outs, args, scratch=(), flops=0, size=0, name=None):
    return pl.pallas_call(
        kernel,
        out_shape=[jax.ShapeDtypeStruct(shape, F32) for shape in outs],
        in_specs=[pl.BlockSpec(memory_space=VMEM)] * len(args),
        out_specs=[pl.BlockSpec(memory_space=VMEM)] * len(outs),
        scratch_shapes=list(scratch),
        compiler_params=pltpu.CompilerParams(vmem_limit_bytes=LIMIT),
        cost_estimate=pl.CostEstimate(flops=flops, bytes_accessed=size, transcendentals=0),
        name=name,
    )(*args)


def place():
    spot = lax.axis_index("dp")
    return spot, lax.axis_index("rep"), spot // 4, lax.axis_index("chain")


def forward_kernel(
    desc_ref, meta_ref, first_far, second_far, far_meta, vec_ref,
    own0, own1, rec0, rec1,
    h1_ref, h2_ref, g2_ref, g1_ref, f_ref, x_ref, member_ref, sums_ref,
    w1h, w1l, w2h, w2l,
):
    spot, core, half, chain = place()
    width = w1h.shape[1]
    rows1 = w1h.shape[0] // 16
    rows2 = w2h.shape[0] // 16
    rows = rows1 + rows2
    for far in range(2):
        for other in range(2):
            block = ((own0, own1), (rec0, rec1))[far][other]
            for delta in range(4):
                owner = ((spot ^ (delta + 4 * far)) * 2 + (core ^ other))
                piece = block[delta * rows : delta * rows + rows1, :]
                high, low = split(piece)
                at = pl.ds(pl.multiple_of(owner * rows1, rows1), rows1)
                w1h[at, :] = high
                w1l[at, :] = low
                piece = block[delta * rows + rows1 : (delta + 1) * rows, :]
                high, low = split(piece)
                at = pl.ds(pl.multiple_of(owner * rows2, rows2), rows2)
                w2h[at, :] = high
                w2l[at, :] = low
    atoms = desc_ref.shape[2]
    near = meta_ref[...]
    away = far_meta[...]
    n_near = [near[1:2, 0:1], near[1:2, 1:2]]
    n_far = [away[1:2, 0:1], away[1:2, 1:2]]
    choose = lambda number, yes, no: jnp.where(jnp.broadcast_to(number, yes.shape) > 0.5, yes, no)
    own_desc = [desc_ref[half, 0], desc_ref[half, 1]]
    direct = first_far[...]
    shared = second_far[...]
    even = chain == 0
    far_desc = [jnp.where(even, direct, shared), jnp.where(even, shared, direct)]
    first = lambda own, far: choose(n_near[0], own[0], far[0])
    second = lambda own, far: choose(n_near[1], own[1], choose(n_near[0], far[0], far[1]))
    x0, x1 = first(own_desc, far_desc), second(own_desc, far_desc)
    n0, n1 = first(n_near, n_far), second(n_near, n_far)
    near_ids = near[0:1, :]
    far_ids = away[0:1, :] + 32.0
    pair = lambda row: [row[:, :atoms], row[:, atoms:]]
    id0, id1 = first(pair(near_ids), pair(far_ids)), second(pair(near_ids), pair(far_ids))
    ids = jnp.broadcast_to(jnp.concatenate([id0, id1], axis=1), (128, 2 * atoms)).T[:, 0:128]
    spots = lax.broadcasted_iota(jnp.int32, (atoms, 128), 0).astype(F32)
    live = jnp.concatenate([(spots < n0).astype(F32), (spots < n1).astype(F32)], axis=0)
    lanes = lax.broadcasted_iota(jnp.int32, (2 * atoms, 128), 1).astype(F32)
    member = jnp.where(ids == lanes, live, 0.0)
    member_ref[...] = member

    x = jnp.concatenate([x0, x1], axis=0)
    x_ref[...] = x
    vec = vec_ref[half]
    c1, c2, w3 = vec[0:1, :], vec[1:2, :], vec[2:3, :]
    w1 = (w1h[...], w1l[...])
    w2 = (w2h[...], w2l[...])
    h1 = jnp.tanh(product(split(x), w1, NN) + c1)
    h1_ref[...] = h1
    h2 = jnp.tanh(product(split(h1), w2, NN) + c2)
    h2_ref[...] = h2
    energy = jnp.sum(h2 * w3, axis=1, keepdims=True)
    sums_ref[0:1, :] = jnp.sum(member * energy, axis=0, keepdims=True)
    sums_ref[1:2, :] = jnp.sum(member, axis=0, keepdims=True)
    sums_ref[2:8, :] = jnp.zeros((6, 128), F32)
    g2 = w3 * (1.0 - h2 * h2)
    g2_ref[...] = g2
    g1 = product(split(g2), w2, NT) * (1.0 - h1 * h1)
    g1_ref[...] = g1
    f_ref[...] = product(split(g1), w1, NT)


def force_kernel(mine, theirs, refs, near, member, f_ref, force_near, force_far, adj_ref, pot_ref):
    other = theirs[...]
    lane = lax.broadcasted_iota(jnp.int32, other.shape, 1)
    other = jnp.where(lane < 32, pltpu.roll(other, 96, 1), pltpu.roll(other, 32, 1))
    total = mine[0:1, :] + other[0:1, :]
    count = jnp.maximum(mine[1:2, :] + other[1:2, :], 1.0)
    error = total / count - refs[0:1, :]
    inside = lax.broadcasted_iota(jnp.int32, (1, 128), 1) < 64
    error = jnp.where(inside, error, 0.0)
    square = error * error
    low = jnp.sum(square[:, 0:32], axis=1, keepdims=True)
    high = jnp.sum(square[:, 32:64], axis=1, keepdims=True)
    pot_ref[...] = jnp.broadcast_to((low + high) / (2.0 * NOISE_VAR), (8, 128))
    scale = error / count / NOISE_VAR
    adj = jnp.sum(member[...] * scale, axis=1, keepdims=True)
    adj_ref[...] = jnp.broadcast_to(adj, adj_ref.shape)
    force = adj * f_ref[...]
    atoms = force.shape[0] // 2
    f0, f1 = force[:atoms], force[atoms:]
    has0 = jnp.broadcast_to(near[1:2, 0:1], f0.shape) > 0.5
    has1 = jnp.broadcast_to(near[1:2, 1:2], f0.shape) > 0.5
    force_near[0] = jnp.where(has0, f0, 0.0)
    force_near[1] = jnp.where(has1, f1, 0.0)
    force_far[0] = jnp.where(has0, jnp.where(has1, 0.0, f1), f0)
    force_far[1] = jnp.where(has0, 0.0, f1)


def gradient_kernel(adj_ref, pot_ref, h1_ref, h2_ref, g2_ref, g1_ref, x_ref, keep, give, dw1, dw2):
    spot, core, half, chain = place()
    adj = adj_ref[...][:, 0:1]
    g2 = adj * g2_ref[...]
    g1 = adj * g1_ref[...]
    dw2[...] = product(split(h1_ref[...]), split(g2), TN)
    dw1[...] = product(split(x_ref[...]), split(g1), TN)
    rows1 = dw1.shape[0] // 16
    rows2 = dw2.shape[0] // 16
    rows = rows1 + rows2
    for delta in range(8):
        for out, holder in ((keep, core), (give, 1 - core)):
            owner = (spot ^ delta) * 2 + holder
            base = delta * rows
            at = pl.ds(pl.multiple_of(owner * rows1, rows1), rows1)
            out[base : base + rows1, :] = dw1[at, :]
            at = pl.ds(pl.multiple_of(owner * rows2, rows2), rows2)
            out[base + rows1 : base + rows, :] = dw2[at, :]
    base = 8 * rows
    width = g2.shape[1]
    vec = [
        jnp.sum(g1, axis=0, keepdims=True),
        jnp.sum(g2, axis=0, keepdims=True),
        jnp.sum(adj * h2_ref[...], axis=0, keepdims=True),
        jnp.broadcast_to(pot_ref[0:1, 0:1], (1, width)),
    ]
    tail = jnp.concatenate(vec + [jnp.zeros((4, width), F32)], axis=0)
    keep[base : base + 8, :] = tail
    give[base : base + 8, :] = tail


def core_sum_kernel(keep, came, s0, s1, s2, s3, o0, o1, o2, o3):
    rows = s0.shape[0]
    for delta, out in enumerate((s0, s1, s2, s3, o0, o1, o2, o3)):
        at = slice(delta * rows, (delta + 1) * rows)
        out[0:rows, :] = keep[at, :] + came[at, :]
        if delta >= 4:
            at = slice(8 * rows, 8 * rows + 8)
            out[rows : rows + 8, :] = keep[at, :] + came[at, :]


def four_sum_kernel(a, b, c, d, out):
    out[...] = (a[...] + b[...]) + (c[...] + d[...])


def flip(axis, delta, size):
    return lambda x: lax.ppermute(x, axis, [(i, i ^ delta) for i in range(size)])


def halves(
    descriptors, counts, struct_ids, ref_energy, first_layer, second_layer, vectors,
    first_momentum, second_momentum, vector_momentum,
):
    nelem, slots, atoms, width = descriptors.shape
    hidden = vectors.shape[2]
    structs = ref_energy.shape[0]
    spot, core, half, chain = place()
    to = [None] + [flip("dp", delta, 8) for delta in range(1, 8)]
    to_core = flip("rep", 1, 2)
    to_chain = flip("chain", 1, 2)
    rows1 = first_layer.shape[1] // hidden
    rows2 = second_layer.shape[1] // hidden
    rows = rows1 + rows2
    shards = jnp.concatenate(
        [first_layer.reshape(nelem, rows1, hidden), second_layer.reshape(nelem, rows2, hidden)], axis=1
    )
    pick = lambda x, at: lax.dynamic_index_in_dim(x, at, 0, keepdims=False)
    own = pick(shards, half)
    got = to[4](pick(shards, 1 - half))

    def meta_of(at):
        ids = pick(struct_ids, at).astype(F32).reshape(1, slots * atoms)
        number = jnp.pad(pick(counts, at).astype(F32).reshape(1, slots), ((0, 0), (0, slots * atoms - slots)))
        refs = jnp.pad(ref_energy.reshape(1, structs), ((0, 0), (0, slots * atoms - structs)))
        return jnp.concatenate([ids, number, refs, jnp.zeros((5, slots * atoms), F32)], axis=0)

    meta = meta_of(half)
    sent_desc = lax.dynamic_slice(descriptors, (1 - half, chain, 0, 0), (1, 1, atoms, width)).reshape(atoms, width)
    message = to[4](jnp.concatenate([sent_desc, meta_of(1 - half)], axis=0))
    direct = message[:atoms]
    far_meta = message[atoms:]
    shared = to_chain(direct)
    own_set = jnp.concatenate([own] + [to[delta](own) for delta in (1, 2, 3)], axis=0)
    own_across = to_core(own_set)
    got_set = jnp.concatenate([got] + [to[delta](got) for delta in (1, 2, 3)], axis=0)
    got_across = to_core(got_set)

    work = slots * atoms
    h1, h2, g2, g1, f, x, member, sums = call(
        forward_kernel,
        [(work, hidden)] * 4 + [(work, width)] * 2 + [(work, 128), (8, 128)],
        (descriptors, meta, direct, shared, far_meta, vectors, own_set, own_across, got_set, got_across),
        scratch=[pltpu.VMEM((width, hidden), BF16)] * 2 + [pltpu.VMEM((hidden, hidden), BF16)] * 2,
        flops=12 * work * hidden * (width + hidden),
        size=8 * 1024 * 1024,
        name="forward",
    )
    refs = jnp.concatenate([meta[2:3, 0:structs], far_meta[2:3, 0:structs], jnp.zeros((1, 128 - 2 * structs), F32)], axis=1)
    force_near, force_far, adj, pot = call(
        force_kernel,
        [(slots, atoms, width)] * 2 + [(work, 128), (8, 128)],
        (sums, to[4](sums), refs, meta, member, f),
        size=2 * 1024 * 1024,
        name="force",
    )
    force_came = to[4](force_far)
    total_rows = 8 * rows + 8
    keep, give = call(
        gradient_kernel,
        [(total_rows, hidden)] * 2,
        (adj, pot, h1, h2, g2, g1, x),
        scratch=[pltpu.VMEM((width, hidden), F32), pltpu.VMEM((hidden, hidden), F32)],
        flops=6 * work * hidden * (width + hidden),
        size=4 * 1024 * 1024,
        name="gradient",
    )
    parts = call(
        core_sum_kernel,
        [(rows, hidden)] * 4 + [(rows + 8, hidden)] * 4,
        (keep, to_core(give)),
        size=3 * 1024 * 1024,
        name="core_sum",
    )
    beyond = [parts[4]] + [to[delta](parts[4 + delta]) for delta in (1, 2, 3)]
    (beyond_sum,) = call(four_sum_kernel, [(rows + 8, hidden)], beyond, size=500 * 1024, name="beyond_sum")
    came = to[4](beyond_sum)
    mine = [parts[0]] + [to[delta](parts[delta]) for delta in (1, 2, 3)]
    (mine_sum,) = call(four_sum_kernel, [(rows, hidden)], mine, size=500 * 1024, name="mine_sum")

    low = half == 0
    order = lambda a, b: jnp.where(low, jnp.stack([a, b]), jnp.stack([b, a]))
    grads = order(mine_sum, came[:rows])
    tails = order(beyond_sum[rows:], came[rows:])
    share_first = grads[:, :rows1].reshape(nelem, rows1 * hidden)
    share_second = grads[:, rows1:].reshape(nelem, rows2 * hidden)
    grad_vectors = tails[:, 0:3, :]
    potential_sum = beyond_sum[rows + 3, 0:1]
    force_partials = order(force_near, force_came)
    new_first_mom = first_momentum - STEP_SIZE * share_first
    new_second_mom = second_momentum - STEP_SIZE * share_second
    new_vector_mom = vector_momentum - STEP_SIZE * grad_vectors
    new_first = first_layer + STEP_SIZE * new_first_mom
    new_second = second_layer + STEP_SIZE * new_second_mom
    new_vectors = vectors + STEP_SIZE * new_vector_mom
    potential = potential_sum / (structs * 16)
    return (
        new_first, new_second, new_vectors, new_first_mom, new_second_mom, new_vector_mom, potential, force_partials,
    )


def element_energies(first, second, vectors, desc):
    lower = jnp.einsum("erf,efj->erj", desc, first, precision=HIGH) + vectors[:, 0][:, None, :]
    hidden = jnp.tanh(lower)
    upper = jnp.einsum("erj,ejk->erk", hidden, second, precision=HIGH) + vectors[:, 1][:, None, :]
    top = jnp.tanh(upper)
    return jnp.einsum("erk,ek->er", top, vectors[:, 2], precision=HIGH)


def structure_terms(energies, live, ids, refs):
    member = (
        ids[..., None] == jnp.arange(refs.shape[0], dtype=jnp.int32)[None, None, None, :]
    ).astype(jnp.float32)
    total = jnp.einsum("ebas,eba->s", member, energies, precision=HIGH)
    count = jnp.maximum(jnp.einsum("ebas,eba->s", member, live, precision=HIGH), 1.0)
    error = total / count - refs
    potential_part = jnp.sum(error * error) / (2.0 * NOISE_VAR)
    scale = error / count / NOISE_VAR
    adjoint = jnp.einsum("ebas,s->eba", member, scale, precision=HIGH) * live
    return (potential_part, adjoint)


def on_device(
    descriptors,
    counts,
    struct_ids,
    ref_energy,
    first_layer,
    second_layer,
    vectors,
    first_momentum,
    second_momentum,
    vector_momentum,
):
    nelem, slots, atoms, width = descriptors.shape
    hidden_width = vectors.shape[2]
    flat_first, flat_second = (
        lax.all_gather(first_layer, ("dp", "rep"), axis=1, tiled=True),
        lax.all_gather(second_layer, ("dp", "rep"), axis=1, tiled=True),
    )
    params = (
        flat_first.reshape(nelem, width, hidden_width),
        flat_second.reshape(nelem, hidden_width, hidden_width),
        vectors,
    )
    positions = jnp.arange(atoms, dtype=jnp.int32)
    live = (positions[None, None, :] < counts[:, :, None]).astype(jnp.float32)

    def forward(block):
        number = block.shape[1]

        def energy_fn(weights, pieces):
            flat = pieces.reshape(nelem, number * atoms, width)
            return element_energies(weights[0], weights[1], weights[2], flat).reshape(
                nelem, number, atoms
            )

        return jax.vjp(energy_fn, params, block)

    raw, pull = forward(descriptors)
    potential_part, adjoint = structure_terms(raw * live, live, struct_ids, ref_energy)
    grads, force_partials = pull(adjoint)
    grad_first = grads[0].reshape(nelem, width * hidden_width)
    grad_second = grads[1].reshape(nelem, hidden_width * hidden_width)
    sum_first, sum_second, grad_vectors, potential_sum = lax.psum(
        (grad_first, grad_second, grads[2], potential_part), ("dp", "rep")
    )
    position = lax.axis_index(("dp", "rep"))
    share_first = lax.dynamic_slice_in_dim(
        sum_first, position * first_layer.shape[1], first_layer.shape[1], 1
    )
    share_second = lax.dynamic_slice_in_dim(
        sum_second, position * second_layer.shape[1], second_layer.shape[1], 1
    )
    new_first_mom = first_momentum - STEP_SIZE * share_first
    new_second_mom = second_momentum - STEP_SIZE * share_second
    new_vector_mom = vector_momentum - STEP_SIZE * grad_vectors
    new_first = first_layer + STEP_SIZE * new_first_mom
    new_second = second_layer + STEP_SIZE * new_second_mom
    new_vectors = vectors + STEP_SIZE * new_vector_mom
    potential = (potential_sum / (ref_energy.shape[0] * lax.axis_size(("dp", "rep")))).reshape(1)
    return (
        new_first,
        new_second,
        new_vectors,
        new_first_mom,
        new_second_mom,
        new_vector_mom,
        potential,
        force_partials,
    )


def solution(mesh):
    placed = (
        P(None, ("dp", "rep"), None, None),
        P(None, ("dp", "rep")),
        P(None, ("dp", "rep"), None),
        P(("dp", "rep")),
        P("chain", ("dp", "rep")),
        P("chain", ("dp", "rep")),
        P("chain", None, None),
        P("chain", ("dp", "rep")),
        P("chain", ("dp", "rep")),
        P("chain", None, None),
    )
    split_by_half = (mesh.shape["chain"], mesh.shape["dp"], mesh.shape["rep"]) == (2, 8, 2)
    return jax.shard_map(
        halves if split_by_half else on_device,
        mesh=mesh,
        in_specs=placed,
        out_specs=(
            P("chain", ("dp", "rep")),
            P("chain", ("dp", "rep")),
            P("chain", None, None),
            P("chain", ("dp", "rep")),
            P("chain", ("dp", "rep")),
            P("chain", None, None),
            P("chain"),
            P("chain", ("dp", "rep"), None, None),
        ),
        check_vma=False,
    )
```

```python
import jax
import jax.numpy as jnp
from jax import lax
from jax.experimental import pallas as pl
from jax.experimental.pallas import tpu as pltpu
from jax.sharding import PartitionSpec as P

NOISE_VAR = 0.1
STEP_SIZE = 0.01
HIGH = lax.Precision.HIGHEST
F32 = jnp.float32
BF16 = jnp.bfloat16
VMEM = pltpu.VMEM
LIMIT = 32 * 1024 * 1024

NT = (((1,), (1,)), ((), ()))
TN = (((0,), (0,)), ((), ()))
NN = (((1,), (0,)), ((), ()))


def split(x):
    high = x.astype(BF16)
    return high, (x - high.astype(F32)).astype(BF16)


def product(left, right, dims):
    one = lambda a, b: lax.dot_general(a, b, dims, preferred_element_type=F32)
    return one(left[0], right[0]) + (one(left[0], right[1]) + one(left[1], right[0]))


def call(kernel, outs, args, scratch=(), flops=0, size=0, name=None):
    return pl.pallas_call(
        kernel,
        out_shape=[jax.ShapeDtypeStruct(shape, kind) for shape, kind in ((*out, F32)[:2] for out in outs)],
        in_specs=[pl.BlockSpec(memory_space=VMEM)] * len(args),
        out_specs=[pl.BlockSpec(memory_space=VMEM)] * len(outs),
        scratch_shapes=list(scratch),
        compiler_params=pltpu.CompilerParams(vmem_limit_bytes=LIMIT),
        cost_estimate=pl.CostEstimate(flops=1, bytes_accessed=1, transcendentals=0),
        name=name,
    )(*args)


def place():
    spot = lax.axis_index("dp")
    return spot, lax.axis_index("rep"), spot // 4, lax.axis_index("chain")


def forward_kernel(
    desc_ref, meta_ref, first_far, second_far, far_meta, vec_ref,
    own0, own1, rec0, rec1,
    h1_ref, h2_ref, x_ref, member_ref, sums_ref, w1h, w1l, w2h, w2l,
):
    spot, core, half, chain = place()
    width = w1h.shape[1]
    rows1 = w1h.shape[0] // 16
    rows2 = w2h.shape[0] // 16
    rows = rows1 + rows2
    for far in range(2):
        for other in range(2):
            block = ((own0, own1), (rec0, rec1))[far][other]
            for delta in range(4):
                owner = ((spot ^ (delta + 4 * far)) * 2 + (core ^ other))
                piece = block[delta * rows : delta * rows + rows1, :]
                high, low = split(piece)
                at = pl.ds(pl.multiple_of(owner * rows1, rows1), rows1)
                w1h[at, :] = high
                w1l[at, :] = low
                piece = block[delta * rows + rows1 : (delta + 1) * rows, :]
                high, low = split(piece)
                at = pl.ds(pl.multiple_of(owner * rows2, rows2), rows2)
                w2h[at, :] = high
                w2l[at, :] = low
    atoms = desc_ref.shape[2]
    near = meta_ref[...]
    away = far_meta[...]
    n_near = [near[1:2, 0:1], near[1:2, 1:2]]
    n_far = [away[1:2, 0:1], away[1:2, 1:2]]
    choose = lambda number, yes, no: jnp.where(jnp.broadcast_to(number, yes.shape) > 0.5, yes, no)
    own_desc = [desc_ref[half, 0], desc_ref[half, 1]]
    direct = first_far[...]
    shared = second_far[...]
    even = chain == 0
    far_desc = [jnp.where(even, direct, shared), jnp.where(even, shared, direct)]
    first = lambda own, far: choose(n_near[0], own[0], far[0])
    second = lambda own, far: choose(n_near[1], own[1], choose(n_near[0], far[0], far[1]))
    x0, x1 = first(own_desc, far_desc), second(own_desc, far_desc)
    n0, n1 = first(n_near, n_far), second(n_near, n_far)
    near_ids = near[0:1, :]
    far_ids = away[0:1, :] + 32.0
    pair = lambda row: [row[:, :atoms], row[:, atoms:]]
    id0, id1 = first(pair(near_ids), pair(far_ids)), second(pair(near_ids), pair(far_ids))
    ids = jnp.broadcast_to(jnp.concatenate([id0, id1], axis=1), (128, 2 * atoms)).T[:, 0:128]
    spots = lax.broadcasted_iota(jnp.int32, (atoms, 128), 0).astype(F32)
    live = jnp.concatenate([(spots < n0).astype(F32), (spots < n1).astype(F32)], axis=0)
    lanes = lax.broadcasted_iota(jnp.int32, (2 * atoms, 128), 1).astype(F32)
    member = jnp.where(ids == lanes, live, 0.0)
    member_ref[...] = member

    x = jnp.concatenate([x0, x1], axis=0)
    x_ref[...] = x
    c1, c2, w3 = [vec_ref[kind, pl.ds(half, 1), :] for kind in range(3)]
    w1 = (w1h[...], w1l[...])
    w2 = (w2h[...], w2l[...])
    h1 = jnp.tanh(product(split(x), w1, NN) + c1)
    h1_ref[...] = h1
    h2 = jnp.tanh(product(split(h1), w2, NN) + c2)
    h2_ref[...] = h2
    energy = jnp.sum(h2 * w3, axis=1, keepdims=True)
    sums_ref[0:1, :] = jnp.sum(member * energy, axis=0, keepdims=True)
    sums_ref[1:2, :] = jnp.sum(member, axis=0, keepdims=True)
    sums_ref[2:8, :] = jnp.zeros((6, 128), F32)


def backward_kernel(h1_ref, h2_ref, vec_ref, w1h, w1l, w2h, w2l, g2_ref, g1_ref, f_ref):
    spot, core, half, chain = place()
    w3 = vec_ref[2, pl.ds(half, 1), :]
    h1, h2 = h1_ref[...], h2_ref[...]
    g2 = w3 * (1.0 - h2 * h2)
    g2_ref[...] = g2
    g1 = product(split(g2), (w2h[...], w2l[...]), NT) * (1.0 - h1 * h1)
    g1_ref[...] = g1
    f_ref[...] = product(split(g1), (w1h[...], w1l[...]), NT)


def force_kernel(mine, theirs, refs, near, member, f_ref, force_near, force_far, adj_ref, pot_ref):
    other = theirs[...]
    lane = lax.broadcasted_iota(jnp.int32, other.shape, 1)
    other = jnp.where(lane < 32, pltpu.roll(other, 96, 1), pltpu.roll(other, 32, 1))
    total = mine[0:1, :] + other[0:1, :]
    count = jnp.maximum(mine[1:2, :] + other[1:2, :], 1.0)
    error = total / count - refs[0:1, :]
    inside = lax.broadcasted_iota(jnp.int32, (1, 128), 1) < 64
    error = jnp.where(inside, error, 0.0)
    square = error * error
    low = jnp.sum(square[:, 0:32], axis=1, keepdims=True)
    high = jnp.sum(square[:, 32:64], axis=1, keepdims=True)
    pot_ref[...] = jnp.broadcast_to((low + high) / (2.0 * NOISE_VAR), (8, 128))
    scale = error / count / NOISE_VAR
    adj = jnp.sum(member[...] * scale, axis=1, keepdims=True)
    adj_ref[...] = jnp.broadcast_to(adj, adj_ref.shape)
    force = adj * f_ref[...]
    atoms = force.shape[0] // 2
    f0, f1 = force[:atoms], force[atoms:]
    has0 = jnp.broadcast_to(near[1:2, 0:1], f0.shape) > 0.5
    has1 = jnp.broadcast_to(near[1:2, 1:2], f0.shape) > 0.5
    force_near[0] = jnp.where(has0, f0, 0.0)
    force_near[1] = jnp.where(has1, f1, 0.0)
    force_far[0] = jnp.where(has0, jnp.where(has1, 0.0, f1), f0)
    force_far[1] = jnp.where(has0, 0.0, f1)


def gradient_kernel(
    adj_ref, pot_ref, h1_ref, h2_ref, g2_ref, g1_ref, x_ref, keep_far, give_far, keep_near, give_near, dw1, dw2,
):
    spot, core, half, chain = place()
    adj = adj_ref[...][:, 0:1]
    g2 = adj * g2_ref[...]
    g1 = adj * g1_ref[...]
    dw2[...] = product(split(h1_ref[...]), split(g2), TN)
    dw1[...] = product(split(x_ref[...]), split(g1), TN)
    rows1 = dw1.shape[0] // 16
    rows2 = dw2.shape[0] // 16
    rows = rows1 + rows2
    for far, keep, give in ((4, keep_far, give_far), (0, keep_near, give_near)):
        for index, delta in enumerate((0, 2, 1, 3)):
            for out, holder in ((keep, core), (give, 1 - core)):
                owner = (spot ^ (delta + far)) * 2 + holder
                base = index * rows
                at = pl.ds(pl.multiple_of(owner * rows1, rows1), rows1)
                out[base : base + rows1, :] = dw1[at, :]
                at = pl.ds(pl.multiple_of(owner * rows2, rows2), rows2)
                out[base + rows1 : base + rows, :] = dw2[at, :]
    base = 4 * rows
    width = g2.shape[1]
    vec = [
        jnp.sum(g1, axis=0, keepdims=True),
        jnp.sum(g2, axis=0, keepdims=True),
        jnp.sum(adj * h2_ref[...], axis=0, keepdims=True),
        jnp.broadcast_to(pot_ref[0:1, 0:1], (1, width)),
    ]
    tail = jnp.concatenate(vec + [jnp.zeros((4, width), F32)], axis=0)
    keep_far[base : base + 8, :] = tail
    give_far[base : base + 8, :] = tail


def halving_kernel(keep, came, stay, leave):
    tail = stay.shape[0] % 48
    rows = stay.shape[0] - tail
    stay[0:rows, :] = keep[0:rows, :] + came[0:rows, :]
    leave[0:rows, :] = keep[rows : 2 * rows, :] + came[rows : 2 * rows, :]
    if tail:
        end = keep[2 * rows :, :] + came[2 * rows :, :]
        stay[rows:, :] = end
        leave[rows:, :] = end


def sum_kernel(a, b, out):
    out[...] = a[...] + b[...]


def message_kernel(desc_hbm, counts_hbm, ids_hbm, refs_hbm, message, near, counts, ids, refs, sems):
    spot, core, half, chain = place()
    atoms = message.shape[0] - 8
    loads = [
        pltpu.make_async_copy(source, target, sems.at[index])
        for index, (source, target) in enumerate(
            (
                (counts_hbm, counts),
                (ids_hbm, ids),
                (refs_hbm, refs),
                (desc_hbm.at[1 - half, chain], message.at[pl.ds(0, atoms)]),
            )
        )
    ]
    for load in loads:
        load.start()
    for load in loads:
        load.wait()
    for out, base, element in ((near, 0, half), (message, atoms, 1 - half)):
        out[base : base + 8, :] = jnp.zeros((8, 2 * atoms), F32)
        row = ids[element].astype(F32)
        out[base : base + 1, 0:atoms] = row[0:1]
        out[base : base + 1, atoms:] = row[1:2]
        number = counts[pl.ds(element, 1), :].astype(F32)
        out[base + 1 : base + 2, 0:2] = number
        out[base + 2 : base + 3, 0 : refs.shape[1]] = refs[...]


def final_kernel(
    mine, beyond, came, first, second, vec, first_mom, second_mom, vec_mom, force_near, force_came,
    new_first, new_second, new_vec, new_first_mom, new_second_mom, new_vec_mom, potential, forces,
    flat_first, flat_second, sems,
):
    spot, core, half, chain = place()
    near_copy = pltpu.make_async_copy(force_near, forces.at[half], sems.at[0])
    far_copy = pltpu.make_async_copy(force_came, forces.at[1 - half], sems.at[1])
    near_copy.start()
    far_copy.start()
    hidden = mine.shape[1]
    rows1 = flat_first.shape[1] // hidden
    rows2 = flat_second.shape[1] // hidden
    rows = rows1 + rows2
    for source, element in ((mine, half), (came, 1 - half)):
        for row in range(rows1):
            flat_first[pl.ds(element, 1), row * hidden : (row + 1) * hidden] = source[row : row + 1, :]
        for row in range(rows2):
            flat_second[pl.ds(element, 1), row * hidden : (row + 1) * hidden] = source[rows1 + row : rows1 + row + 1, :]
    for grad, value, momentum, new_value, new_momentum in (
        (flat_first, first, first_mom, new_first, new_first_mom),
        (flat_second, second, second_mom, new_second, new_second_mom),
    ):
        moved = momentum[...] - STEP_SIZE * grad[...]
        new_momentum[...] = moved
        new_value[...] = value[...] + STEP_SIZE * moved
    low = jnp.full((1, hidden), half, jnp.int32) == 0
    for kind in range(3):
        own = beyond[rows + kind : rows + kind + 1, :]
        other = came[rows + kind : rows + kind + 1, :]
        for element in range(2):
            grad = jnp.where(low, own, other) if element == 0 else jnp.where(low, other, own)
            moved = vec_mom[kind, element : element + 1, :] - STEP_SIZE * grad
            new_vec_mom[kind, element : element + 1, :] = moved
            new_vec[kind, element : element + 1, :] = vec[kind, element : element + 1, :] + STEP_SIZE * moved
    potential[...] = beyond[rows + 3 : rows + 4, 0:128] * (1.0 / 512.0)
    near_copy.wait()
    far_copy.wait()


def after(value, *others):
    return lax.optimization_barrier((value,) + others)[0]


def flip(axis, delta, size):
    return lambda x: lax.ppermute(x, axis, [(i, i ^ delta) for i in range(size)])


def halves(
    descriptors, counts, struct_ids, ref_energy, first_layer, second_layer, vectors,
    first_momentum, second_momentum, vector_momentum,
):
    nelem, slots, atoms, width = descriptors.shape
    hidden = vectors.shape[2]
    structs = ref_energy.shape[0]
    spot, core, half, chain = place()
    to = [None] + [flip("dp", delta, 8) for delta in range(1, 8)]
    to_core = flip("rep", 1, 2)
    to_chain = flip("chain", 1, 2)
    rows1 = first_layer.shape[1] // hidden
    rows2 = second_layer.shape[1] // hidden
    rows = rows1 + rows2
    shards = jnp.concatenate(
        [first_layer.reshape(nelem, rows1, hidden), second_layer.reshape(nelem, rows2, hidden)], axis=1
    )
    pick = lambda x, at: lax.dynamic_index_in_dim(x, at, 0, keepdims=False)
    own = pick(shards, half)
    got = to[4](pick(shards, 1 - half))

    any_space = pl.BlockSpec(memory_space=pl.ANY)
    vmem = pl.BlockSpec(memory_space=VMEM)
    message, meta = pl.pallas_call(
        message_kernel,
        out_shape=[jax.ShapeDtypeStruct((atoms + 8, width), F32), jax.ShapeDtypeStruct((8, width), F32)],
        in_specs=[pl.BlockSpec(memory_space=pltpu.HBM)] * 4,
        out_specs=[vmem] * 2,
        scratch_shapes=[
            pltpu.VMEM(counts.shape, jnp.int32), pltpu.VMEM(struct_ids.shape, jnp.int32), pltpu.VMEM((1, structs), F32),
            pltpu.SemaphoreType.DMA((4,)),
        ],
        compiler_params=pltpu.CompilerParams(vmem_limit_bytes=60 * 1024 * 1024),
        name="message",
    )(descriptors, counts, struct_ids, ref_energy.reshape(1, structs))
    message = to[4](message)
    own_came = [to[delta](own) for delta in (1, 2, 3)]
    got = after(got, message, *own_came)
    direct = message[:atoms]
    far_meta = message[atoms:]
    shared = to_chain(direct)
    own_set = jnp.concatenate(lax.optimization_barrier((own, *own_came, got))[:4], axis=0)
    own_across = to_core(own_set)
    got_set = jnp.concatenate([got] + [to[delta](got) for delta in (1, 2, 3)], axis=0)
    got_across = to_core(after(got_set, shared))

    work = slots * atoms
    vec = vectors.transpose(1, 0, 2)
    h1, h2, x, member, sums, *weights = call(
        forward_kernel,
        [((work, hidden),)] * 2 + [((work, width),), ((work, 128),), ((8, 128),)]
        + [((width, hidden), BF16)] * 2 + [((hidden, hidden), BF16)] * 2,
        (descriptors, meta, direct, shared, far_meta, vec, own_set, own_across, got_set, got_across),
        flops=6 * work * hidden * (width + hidden),
        size=6 * 1024 * 1024,
        name="forward",
    )
    sums_came = to[4](sums)
    g2, g1, f = call(
        backward_kernel,
        [((work, hidden),)] * 2 + [((work, width),)],
        (h1, h2, vec, *weights),
        flops=6 * work * hidden * (width + hidden),
        size=6 * 1024 * 1024,
        name="backward",
    )
    refs = jnp.concatenate([meta[2:3, 0:structs], far_meta[2:3, 0:structs], jnp.zeros((1, 128 - 2 * structs), F32)], axis=1)
    force_near, force_far, adj, pot = call(
        force_kernel,
        [((slots, atoms, width),)] * 2 + [((work, 128),), ((8, 128),)],
        (sums, sums_came, refs, meta, member, f),
        size=2 * 1024 * 1024,
        name="force",
    )
    force_came = to[4](force_far)
    tail = 8
    group = 4 * rows
    keep_far, give_far, keep_near, give_near = call(
        gradient_kernel,
        [((group + tail, hidden),)] * 2 + [((group, hidden),)] * 2,
        (adj, pot, h1, h2, g2, g1, x),
        scratch=[pltpu.VMEM((width, hidden), F32), pltpu.VMEM((hidden, hidden), F32)],
        flops=6 * work * hidden * (width + hidden),
        size=4 * 1024 * 1024,
        name="gradient",
    )

    def halve(keep, came, end, name):
        left = (keep.shape[0] - end) // 2 + end
        return call(halving_kernel, [((left, hidden),)] * 2, (keep, came), size=4 * 4 * left * hidden, name=name)

    far_stay, far_leave = halve(keep_far, to_core(give_far), tail, "far_core")
    near_stay, near_leave = halve(keep_near, to_core(give_near), 0, "near_core")
    far_came = to[1](far_leave)
    far_stay, far_leave = halve(far_stay, far_came, tail, "far_x")
    near_came = to[1](after(near_leave, far_came))
    far_came = to[2](far_leave)
    near_stay, near_leave = halve(near_stay, near_came, 0, "near_x")
    (beyond_sum,) = call(sum_kernel, [((rows + tail, hidden),)], (far_stay, far_came), size=400 * 1024, name="far_z")
    came = to[4](after(beyond_sum, force_came))
    (mine_sum,) = call(sum_kernel, [((rows, hidden),)], (near_stay, to[2](near_leave)), size=400 * 1024, name="near_z")
    shape = lambda x: jax.ShapeDtypeStruct(x.shape, F32)
    vec_mom = vector_momentum.transpose(1, 0, 2)
    (
        new_first, new_second, new_vec, new_first_mom, new_second_mom, new_vec_mom, potential, force_partials,
    ) = pl.pallas_call(
        final_kernel,
        out_shape=[
            shape(first_layer), shape(second_layer), shape(vec), shape(first_layer), shape(second_layer), shape(vec),
            jax.ShapeDtypeStruct((1, 128), F32), shape(descriptors),
        ],
        in_specs=[vmem] * 11,
        out_specs=[vmem] * 7 + [any_space],
        scratch_shapes=[
            pltpu.VMEM(first_layer.shape, F32), pltpu.VMEM(second_layer.shape, F32), pltpu.SemaphoreType.DMA((2,)),
        ],
        compiler_params=pltpu.CompilerParams(vmem_limit_bytes=8 * 1024 * 1024),
        name="final",
    )(
        mine_sum, beyond_sum, came, first_layer, second_layer, vec, first_momentum, second_momentum, vec_mom,
        force_near, after(force_came, came, mine_sum),
    )
    return (
        new_first, new_second, new_vec.transpose(1, 0, 2), new_first_mom, new_second_mom,
        new_vec_mom.transpose(1, 0, 2), potential[0, 0:1], force_partials,
    )


def element_energies(first, second, vectors, desc):
    lower = jnp.einsum("erf,efj->erj", desc, first, precision=HIGH) + vectors[:, 0][:, None, :]
    hidden = jnp.tanh(lower)
    upper = jnp.einsum("erj,ejk->erk", hidden, second, precision=HIGH) + vectors[:, 1][:, None, :]
    top = jnp.tanh(upper)
    return jnp.einsum("erk,ek->er", top, vectors[:, 2], precision=HIGH)


def structure_terms(energies, live, ids, refs):
    member = (
        ids[..., None] == jnp.arange(refs.shape[0], dtype=jnp.int32)[None, None, None, :]
    ).astype(jnp.float32)
    total = jnp.einsum("ebas,eba->s", member, energies, precision=HIGH)
    count = jnp.maximum(jnp.einsum("ebas,eba->s", member, live, precision=HIGH), 1.0)
    error = total / count - refs
    potential_part = jnp.sum(error * error) / (2.0 * NOISE_VAR)
    scale = error / count / NOISE_VAR
    adjoint = jnp.einsum("ebas,s->eba", member, scale, precision=HIGH) * live
    return (potential_part, adjoint)


def on_device(
    descriptors,
    counts,
    struct_ids,
    ref_energy,
    first_layer,
    second_layer,
    vectors,
    first_momentum,
    second_momentum,
    vector_momentum,
):
    nelem, slots, atoms, width = descriptors.shape
    hidden_width = vectors.shape[2]
    flat_first, flat_second = (
        lax.all_gather(first_layer, ("dp", "rep"), axis=1, tiled=True),
        lax.all_gather(second_layer, ("dp", "rep"), axis=1, tiled=True),
    )
    params = (
        flat_first.reshape(nelem, width, hidden_width),
        flat_second.reshape(nelem, hidden_width, hidden_width),
        vectors,
    )
    positions = jnp.arange(atoms, dtype=jnp.int32)
    live = (positions[None, None, :] < counts[:, :, None]).astype(jnp.float32)

    def forward(block):
        number = block.shape[1]

        def energy_fn(weights, pieces):
            flat = pieces.reshape(nelem, number * atoms, width)
            return element_energies(weights[0], weights[1], weights[2], flat).reshape(
                nelem, number, atoms
            )

        return jax.vjp(energy_fn, params, block)

    raw, pull = forward(descriptors)
    potential_part, adjoint = structure_terms(raw * live, live, struct_ids, ref_energy)
    grads, force_partials = pull(adjoint)
    grad_first = grads[0].reshape(nelem, width * hidden_width)
    grad_second = grads[1].reshape(nelem, hidden_width * hidden_width)
    sum_first, sum_second, grad_vectors, potential_sum = lax.psum(
        (grad_first, grad_second, grads[2], potential_part), ("dp", "rep")
    )
    position = lax.axis_index(("dp", "rep"))
    share_first = lax.dynamic_slice_in_dim(
        sum_first, position * first_layer.shape[1], first_layer.shape[1], 1
    )
    share_second = lax.dynamic_slice_in_dim(
        sum_second, position * second_layer.shape[1], second_layer.shape[1], 1
    )
    new_first_mom = first_momentum - STEP_SIZE * share_first
    new_second_mom = second_momentum - STEP_SIZE * share_second
    new_vector_mom = vector_momentum - STEP_SIZE * grad_vectors
    new_first = first_layer + STEP_SIZE * new_first_mom
    new_second = second_layer + STEP_SIZE * new_second_mom
    new_vectors = vectors + STEP_SIZE * new_vector_mom
    potential = (potential_sum / (ref_energy.shape[0] * lax.axis_size(("dp", "rep")))).reshape(1)
    return (
        new_first,
        new_second,
        new_vectors,
        new_first_mom,
        new_second_mom,
        new_vector_mom,
        potential,
        force_partials,
    )


def solution(mesh):
    placed = (
        P(None, ("dp", "rep"), None, None),
        P(None, ("dp", "rep")),
        P(None, ("dp", "rep"), None),
        P(("dp", "rep")),
        P("chain", ("dp", "rep")),
        P("chain", ("dp", "rep")),
        P("chain", None, None),
        P("chain", ("dp", "rep")),
        P("chain", ("dp", "rep")),
        P("chain", None, None),
    )
    split_by_half = (mesh.shape["chain"], mesh.shape["dp"], mesh.shape["rep"]) == (2, 8, 2)
    return jax.shard_map(
        halves if split_by_half else on_device,
        mesh=mesh,
        in_specs=placed,
        out_specs=(
            P("chain", ("dp", "rep")),
            P("chain", ("dp", "rep")),
            P("chain", None, None),
            P("chain", ("dp", "rep")),
            P("chain", ("dp", "rep")),
            P("chain", None, None),
            P("chain"),
            P("chain", ("dp", "rep"), None, None),
        ),
        check_vma=False,
    )
```

```python
import jax
import jax.numpy as jnp
from jax import lax
from jax.experimental import pallas as pl
from jax.experimental.pallas import tpu as pltpu
from jax.sharding import PartitionSpec as P

NOISE_VAR = 0.1
STEP_SIZE = 0.01
HIGH = lax.Precision.HIGHEST
F32 = jnp.float32
BF16 = jnp.bfloat16
VMEM = pltpu.VMEM
LIMIT = 32 * 1024 * 1024

NT = (((1,), (1,)), ((), ()))
TN = (((0,), (0,)), ((), ()))
NN = (((1,), (0,)), ((), ()))


def split(x):
    high = x.astype(BF16)
    return high, (x - high.astype(F32)).astype(BF16)


def product(left, right, dims):
    one = lambda a, b: lax.dot_general(a, b, dims, preferred_element_type=F32)
    return one(left[0], right[0]) + (one(left[0], right[1]) + one(left[1], right[0]))


def call(kernel, outs, args, scratch=(), flops=0, size=0, name=None):
    return pl.pallas_call(
        kernel,
        out_shape=[jax.ShapeDtypeStruct(shape, kind) for shape, kind in ((*out, F32)[:2] for out in outs)],
        in_specs=[pl.BlockSpec(memory_space=VMEM)] * len(args),
        out_specs=[pl.BlockSpec(memory_space=VMEM)] * len(outs),
        scratch_shapes=list(scratch),
        compiler_params=pltpu.CompilerParams(vmem_limit_bytes=LIMIT),
        cost_estimate=pl.CostEstimate(flops=1, bytes_accessed=1, transcendentals=0),
        name=name,
    )(*args)


def place():
    spot = lax.axis_index("dp")
    return spot, lax.axis_index("rep"), spot // 4, lax.axis_index("chain")


def forward_kernel(
    desc_ref, meta_ref, first_far, second_far, far_meta, vec_ref,
    own0, own1, rec0, rec1,
    h1_ref, h2_ref, x_ref, member_ref, sums_ref, w1h, w1l, w2h, w2l,
):
    spot, core, half, chain = place()
    width = w1h.shape[1]
    rows1 = w1h.shape[0] // 16
    rows2 = w2h.shape[0] // 16
    rows = rows1 + rows2
    for far in range(2):
        for other in range(2):
            block = ((own0, own1), (rec0, rec1))[far][other]
            for delta in range(4):
                owner = ((spot ^ (delta + 4 * far)) * 2 + (core ^ other))
                piece = block[delta * rows : delta * rows + rows1, :]
                high, low = split(piece)
                at = pl.ds(pl.multiple_of(owner * rows1, rows1), rows1)
                w1h[at, :] = high
                w1l[at, :] = low
                piece = block[delta * rows + rows1 : (delta + 1) * rows, :]
                high, low = split(piece)
                at = pl.ds(pl.multiple_of(owner * rows2, rows2), rows2)
                w2h[at, :] = high
                w2l[at, :] = low
    atoms = desc_ref.shape[2]
    near = meta_ref[...]
    away = far_meta[...]
    n_near = [near[1:2, 0:1], near[1:2, 1:2]]
    n_far = [away[1:2, 0:1], away[1:2, 1:2]]
    choose = lambda number, yes, no: jnp.where(jnp.broadcast_to(number, yes.shape) > 0.5, yes, no)
    own_desc = [desc_ref[half, 0], desc_ref[half, 1]]
    direct = first_far[...]
    shared = second_far[...]
    even = chain == 0
    far_desc = [jnp.where(even, direct, shared), jnp.where(even, shared, direct)]
    first = lambda own, far: choose(n_near[0], own[0], far[0])
    second = lambda own, far: choose(n_near[1], own[1], choose(n_near[0], far[0], far[1]))
    x0, x1 = first(own_desc, far_desc), second(own_desc, far_desc)
    n0, n1 = first(n_near, n_far), second(n_near, n_far)
    near_ids = near[0:1, :]
    far_ids = away[0:1, :] + 32.0
    pair = lambda row: [row[:, :atoms], row[:, atoms:]]
    id0, id1 = first(pair(near_ids), pair(far_ids)), second(pair(near_ids), pair(far_ids))
    ids = jnp.broadcast_to(jnp.concatenate([id0, id1], axis=1), (128, 2 * atoms)).T[:, 0:128]
    spots = lax.broadcasted_iota(jnp.int32, (atoms, 128), 0).astype(F32)
    live = jnp.concatenate([(spots < n0).astype(F32), (spots < n1).astype(F32)], axis=0)
    lanes = lax.broadcasted_iota(jnp.int32, (2 * atoms, 128), 1).astype(F32)
    member = jnp.where(ids == lanes, live, 0.0)
    member_ref[...] = member

    x = jnp.concatenate([x0, x1], axis=0)
    x_ref[...] = x
    c1, c2, w3 = [vec_ref[kind, pl.ds(half, 1), :] for kind in range(3)]
    w1 = (w1h[...], w1l[...])
    w2 = (w2h[...], w2l[...])
    h1 = jnp.tanh(product(split(x), w1, NN) + c1)
    h1_ref[...] = h1
    h2 = jnp.tanh(product(split(h1), w2, NN) + c2)
    h2_ref[...] = h2
    energy = jnp.sum(h2 * w3, axis=1, keepdims=True)
    sums_ref[0:1, :] = jnp.sum(member * energy, axis=0, keepdims=True)
    sums_ref[1:2, :] = jnp.sum(member, axis=0, keepdims=True)
    sums_ref[2:8, :] = jnp.zeros((6, 128), F32)


def backward_kernel(h1_ref, h2_ref, vec_ref, w1h, w1l, w2h, w2l, g2_ref, g1_ref, f_ref):
    spot, core, half, chain = place()
    w3 = vec_ref[2, pl.ds(half, 1), :]
    h1, h2 = h1_ref[...], h2_ref[...]
    g2 = w3 * (1.0 - h2 * h2)
    g2_ref[...] = g2
    g1 = product(split(g2), (w2h[...], w2l[...]), NT) * (1.0 - h1 * h1)
    g1_ref[...] = g1
    f_ref[...] = product(split(g1), (w1h[...], w1l[...]), NT)


def force_kernel(mine, theirs, refs, near, member, f_ref, force_near, force_far, adj_ref, pot_ref):
    other = theirs[...]
    lane = lax.broadcasted_iota(jnp.int32, other.shape, 1)
    other = jnp.where(lane < 32, pltpu.roll(other, 96, 1), pltpu.roll(other, 32, 1))
    total = mine[0:1, :] + other[0:1, :]
    count = jnp.maximum(mine[1:2, :] + other[1:2, :], 1.0)
    error = total / count - refs[0:1, :]
    inside = lax.broadcasted_iota(jnp.int32, (1, 128), 1) < 64
    error = jnp.where(inside, error, 0.0)
    square = error * error
    low = jnp.sum(square[:, 0:32], axis=1, keepdims=True)
    high = jnp.sum(square[:, 32:64], axis=1, keepdims=True)
    pot_ref[...] = jnp.broadcast_to((low + high) / (2.0 * NOISE_VAR), (8, 128))
    scale = error / count / NOISE_VAR
    adj = jnp.sum(member[...] * scale, axis=1, keepdims=True)
    adj_ref[...] = jnp.broadcast_to(adj, adj_ref.shape)
    force = adj * f_ref[...]
    atoms = force.shape[0] // 2
    f0, f1 = force[:atoms], force[atoms:]
    has0 = jnp.broadcast_to(near[1:2, 0:1], f0.shape) > 0.5
    has1 = jnp.broadcast_to(near[1:2, 1:2], f0.shape) > 0.5
    force_near[0] = jnp.where(has0, f0, 0.0)
    force_near[1] = jnp.where(has1, f1, 0.0)
    force_far[0] = jnp.where(has0, jnp.where(has1, 0.0, f1), f0)
    force_far[1] = jnp.where(has0, 0.0, f1)


def gradient_kernel(
    adj_ref, pot_ref, h1_ref, h2_ref, g2_ref, g1_ref, x_ref, keep_far, give_far, keep_near, give_near, dw1, dw2,
):
    spot, core, half, chain = place()
    adj = adj_ref[...][:, 0:1]
    g2 = adj * g2_ref[...]
    g1 = adj * g1_ref[...]
    dw2[...] = product(split(h1_ref[...]), split(g2), TN)
    dw1[...] = product(split(x_ref[...]), split(g1), TN)
    rows1 = dw1.shape[0] // 16
    rows2 = dw2.shape[0] // 16
    rows = rows1 + rows2
    for far, keep, give in ((4, keep_far, give_far), (0, keep_near, give_near)):
        for index, delta in enumerate((0, 2, 1, 3)):
            for out, holder in ((keep, core), (give, 1 - core)):
                owner = (spot ^ (delta + far)) * 2 + holder
                base = index * rows
                at = pl.ds(pl.multiple_of(owner * rows1, rows1), rows1)
                out[base : base + rows1, :] = dw1[at, :]
                at = pl.ds(pl.multiple_of(owner * rows2, rows2), rows2)
                out[base + rows1 : base + rows, :] = dw2[at, :]
    base = 4 * rows
    width = g2.shape[1]
    vec = [
        jnp.sum(g1, axis=0, keepdims=True),
        jnp.sum(g2, axis=0, keepdims=True),
        jnp.sum(adj * h2_ref[...], axis=0, keepdims=True),
        jnp.broadcast_to(pot_ref[0:1, 0:1], (1, width)),
    ]
    tail = jnp.concatenate(vec + [jnp.zeros((4, width), F32)], axis=0)
    keep_far[base : base + 8, :] = tail
    give_far[base : base + 8, :] = tail


def halving_kernel(keep, came, stay, leave):
    tail = stay.shape[0] % 48
    rows = stay.shape[0] - tail
    stay[0:rows, :] = keep[0:rows, :] + came[0:rows, :]
    leave[0:rows, :] = keep[rows : 2 * rows, :] + came[rows : 2 * rows, :]
    if tail:
        end = keep[2 * rows :, :] + came[2 * rows :, :]
        stay[rows:, :] = end
        leave[rows:, :] = end


def sum_kernel(a, b, *rest):
    out = rest[-1]
    out[...] = a[...] + b[...]


def message_kernel(desc_hbm, counts_hbm, ids_hbm, refs_hbm, message, near, counts, ids, refs, sems):
    spot, core, half, chain = place()
    atoms = message.shape[0] - 8
    loads = [
        pltpu.make_async_copy(source, target, sems.at[index])
        for index, (source, target) in enumerate(
            (
                (counts_hbm, counts),
                (ids_hbm, ids),
                (refs_hbm, refs),
                (desc_hbm.at[1 - half, chain], message.at[pl.ds(0, atoms)]),
            )
        )
    ]
    for load in loads:
        load.start()
    for load in loads:
        load.wait()
    for out, base, element in ((near, 0, half), (message, atoms, 1 - half)):
        out[base : base + 8, :] = jnp.zeros((8, 2 * atoms), F32)
        row = ids[element].astype(F32)
        out[base : base + 1, 0:atoms] = row[0:1]
        out[base : base + 1, atoms:] = row[1:2]
        number = counts[pl.ds(element, 1), :].astype(F32)
        out[base + 1 : base + 2, 0:2] = number
        out[base + 2 : base + 3, 0 : refs.shape[1]] = refs[...]


def final_kernel(
    mine, beyond, came, first, second, vec, first_mom, second_mom, vec_mom, force_near, force_came,
    new_first, new_second, new_vec, new_first_mom, new_second_mom, new_vec_mom, potential, forces,
    flat_first, flat_second, sems,
):
    spot, core, half, chain = place()
    near_copy = pltpu.make_async_copy(force_near, forces.at[half], sems.at[0])
    far_copy = pltpu.make_async_copy(force_came, forces.at[1 - half], sems.at[1])
    near_copy.start()
    far_copy.start()
    hidden = mine.shape[1]
    rows1 = flat_first.shape[1] // hidden
    rows2 = flat_second.shape[1] // hidden
    rows = rows1 + rows2
    for source, element in ((mine, half), (came, 1 - half)):
        for row in range(rows1):
            flat_first[pl.ds(element, 1), row * hidden : (row + 1) * hidden] = source[row : row + 1, :]
        for row in range(rows2):
            flat_second[pl.ds(element, 1), row * hidden : (row + 1) * hidden] = source[rows1 + row : rows1 + row + 1, :]
    for grad, value, momentum, new_value, new_momentum in (
        (flat_first, first, first_mom, new_first, new_first_mom),
        (flat_second, second, second_mom, new_second, new_second_mom),
    ):
        moved = momentum[...] - STEP_SIZE * grad[...]
        new_momentum[...] = moved
        new_value[...] = value[...] + STEP_SIZE * moved
    low = jnp.full((1, hidden), half, jnp.int32) == 0
    for kind in range(3):
        own = beyond[rows + kind : rows + kind + 1, :]
        other = came[rows + kind : rows + kind + 1, :]
        for element in range(2):
            grad = jnp.where(low, own, other) if element == 0 else jnp.where(low, other, own)
            moved = vec_mom[kind, element : element + 1, :] - STEP_SIZE * grad
            new_vec_mom[kind, element : element + 1, :] = moved
            new_vec[kind, element : element + 1, :] = vec[kind, element : element + 1, :] + STEP_SIZE * moved
    potential[...] = beyond[rows + 3 : rows + 4, 0:128] * (1.0 / 512.0)
    near_copy.wait()
    far_copy.wait()


def after(value, *others):
    return lax.optimization_barrier((value,) + others)[0]


def flip(axis, delta, size):
    return lambda x: lax.ppermute(x, axis, [(i, i ^ delta) for i in range(size)])


def halves(
    descriptors, counts, struct_ids, ref_energy, first_layer, second_layer, vectors,
    first_momentum, second_momentum, vector_momentum,
):
    nelem, slots, atoms, width = descriptors.shape
    hidden = vectors.shape[2]
    structs = ref_energy.shape[0]
    spot, core, half, chain = place()
    to = [None] + [flip("dp", delta, 8) for delta in range(1, 8)]
    to_core = flip("rep", 1, 2)
    to_chain = flip("chain", 1, 2)
    rows1 = first_layer.shape[1] // hidden
    rows2 = second_layer.shape[1] // hidden
    rows = rows1 + rows2
    shards = jnp.concatenate(
        [first_layer.reshape(nelem, rows1, hidden), second_layer.reshape(nelem, rows2, hidden)], axis=1
    )
    pick = lambda x, at: lax.dynamic_index_in_dim(x, at, 0, keepdims=False)
    own = pick(shards, half)
    got = to[4](pick(shards, 1 - half))

    any_space = pl.BlockSpec(memory_space=pl.ANY)
    vmem = pl.BlockSpec(memory_space=VMEM)
    message, meta = pl.pallas_call(
        message_kernel,
        out_shape=[jax.ShapeDtypeStruct((atoms + 8, width), F32), jax.ShapeDtypeStruct((8, width), F32)],
        in_specs=[pl.BlockSpec(memory_space=pltpu.HBM)] * 4,
        out_specs=[vmem] * 2,
        scratch_shapes=[
            pltpu.VMEM(counts.shape, jnp.int32), pltpu.VMEM(struct_ids.shape, jnp.int32), pltpu.VMEM((1, structs), F32),
            pltpu.SemaphoreType.DMA((4,)),
        ],
        compiler_params=pltpu.CompilerParams(vmem_limit_bytes=4 * 1024 * 1024),
        name="message",
    )(descriptors, counts, struct_ids, ref_energy.reshape(1, structs))
    message = to[4](message)
    own_z = to[2](own)
    own_x = to[1](jnp.concatenate([own, own_z]))
    own_came = [own_x[:rows], own_z, own_x[rows:]]
    got = after(got, own)
    direct = message[:atoms]
    far_meta = message[atoms:]
    shared = to_chain(direct)
    own_set = jnp.concatenate(lax.optimization_barrier((own, *own_came, got))[:4], axis=0)
    own_across = to_core(own_set)
    got_z = to[2](got)
    got_x = to[1](jnp.concatenate([got, got_z]))
    got_set = jnp.concatenate([got, got_x[:rows], got_z, got_x[rows:]], axis=0)
    got_across = to_core(after(got_set, shared))

    work = slots * atoms
    vec = vectors.transpose(1, 0, 2)
    h1, h2, x, member, sums, *weights = call(
        forward_kernel,
        [((work, hidden),)] * 2 + [((work, width),), ((work, 128),), ((8, 128),)]
        + [((width, hidden), BF16)] * 2 + [((hidden, hidden), BF16)] * 2,
        (descriptors, meta, direct, shared, far_meta, vec, own_set, own_across, got_set, got_across),
        flops=6 * work * hidden * (width + hidden),
        size=6 * 1024 * 1024,
        name="forward",
    )
    sums_came = to[4](sums)
    g2, g1, f = call(
        backward_kernel,
        [((work, hidden),)] * 2 + [((work, width),)],
        (h1, h2, vec, *weights),
        flops=6 * work * hidden * (width + hidden),
        size=6 * 1024 * 1024,
        name="backward",
    )
    refs = jnp.concatenate([meta[2:3, 0:structs], far_meta[2:3, 0:structs], jnp.zeros((1, 128 - 2 * structs), F32)], axis=1)
    force_near, force_far, adj, pot = call(
        force_kernel,
        [((slots, atoms, width),)] * 2 + [((work, 128),), ((8, 128),)],
        (sums, sums_came, refs, meta, member, f),
        size=2 * 1024 * 1024,
        name="force",
    )
    force_came = to[4](force_far)
    tail = 8
    group = 4 * rows
    keep_far, give_far, keep_near, give_near = call(
        gradient_kernel,
        [((group + tail, hidden),)] * 2 + [((group, hidden),)] * 2,
        (adj, pot, h1, h2, g2, g1, x),
        scratch=[pltpu.VMEM((width, hidden), F32), pltpu.VMEM((hidden, hidden), F32)],
        flops=6 * work * hidden * (width + hidden),
        size=4 * 1024 * 1024,
        name="gradient",
    )

    def halve(keep, came, end, name):
        left = (keep.shape[0] - end) // 2 + end
        return call(halving_kernel, [((left, hidden),)] * 2, (keep, came), size=4 * 4 * left * hidden, name=name)

    far_stay, far_leave = halve(keep_far, to_core(give_far), tail, "far_core")
    near_stay, near_leave = halve(keep_near, to_core(give_near), 0, "near_core")
    far_came = to[1](far_leave)
    far_stay, far_leave = halve(far_stay, far_came, tail, "far_x")
    near_came = to[1](after(near_leave, far_came))
    far_came = to[2](far_leave)
    near_stay, near_leave = halve(near_stay, near_came, 0, "near_x")
    token = force_came[0, 0:8, 0:128]
    token = to_core(token)
    (beyond_sum,) = call(sum_kernel, [((rows + tail, hidden),)], (far_stay, far_came, token), name="far_z")
    came = to[4](beyond_sum)
    (mine_sum,) = call(sum_kernel, [((rows, hidden),)], (near_stay, to[2](near_leave)), size=400 * 1024, name="near_z")
    shape = lambda x: jax.ShapeDtypeStruct(x.shape, F32)
    vec_mom = vector_momentum.transpose(1, 0, 2)
    (
        new_first, new_second, new_vec, new_first_mom, new_second_mom, new_vec_mom, potential, force_partials,
    ) = pl.pallas_call(
        final_kernel,
        out_shape=[
            shape(first_layer), shape(second_layer), shape(vec), shape(first_layer), shape(second_layer), shape(vec),
            jax.ShapeDtypeStruct((1, 128), F32), shape(descriptors),
        ],
        in_specs=[vmem] * 11,
        out_specs=[vmem] * 7 + [any_space],
        scratch_shapes=[
            pltpu.VMEM(first_layer.shape, F32), pltpu.VMEM(second_layer.shape, F32), pltpu.SemaphoreType.DMA((2,)),
        ],
        compiler_params=pltpu.CompilerParams(vmem_limit_bytes=8 * 1024 * 1024),
        name="final",
    )(
        mine_sum, beyond_sum, came, first_layer, second_layer, vec, first_momentum, second_momentum, vec_mom,
        force_near, after(force_came, came, mine_sum),
    )
    return (
        new_first, new_second, new_vec.transpose(1, 0, 2), new_first_mom, new_second_mom,
        new_vec_mom.transpose(1, 0, 2), potential[0, 0:1], force_partials,
    )


def element_energies(first, second, vectors, desc):
    lower = jnp.einsum("erf,efj->erj", desc, first, precision=HIGH) + vectors[:, 0][:, None, :]
    hidden = jnp.tanh(lower)
    upper = jnp.einsum("erj,ejk->erk", hidden, second, precision=HIGH) + vectors[:, 1][:, None, :]
    top = jnp.tanh(upper)
    return jnp.einsum("erk,ek->er", top, vectors[:, 2], precision=HIGH)


def structure_terms(energies, live, ids, refs):
    member = (
        ids[..., None] == jnp.arange(refs.shape[0], dtype=jnp.int32)[None, None, None, :]
    ).astype(jnp.float32)
    total = jnp.einsum("ebas,eba->s", member, energies, precision=HIGH)
    count = jnp.maximum(jnp.einsum("ebas,eba->s", member, live, precision=HIGH), 1.0)
    error = total / count - refs
    potential_part = jnp.sum(error * error) / (2.0 * NOISE_VAR)
    scale = error / count / NOISE_VAR
    adjoint = jnp.einsum("ebas,s->eba", member, scale, precision=HIGH) * live
    return (potential_part, adjoint)


def on_device(
    descriptors,
    counts,
    struct_ids,
    ref_energy,
    first_layer,
    second_layer,
    vectors,
    first_momentum,
    second_momentum,
    vector_momentum,
):
    nelem, slots, atoms, width = descriptors.shape
    hidden_width = vectors.shape[2]
    flat_first, flat_second = (
        lax.all_gather(first_layer, ("dp", "rep"), axis=1, tiled=True),
        lax.all_gather(second_layer, ("dp", "rep"), axis=1, tiled=True),
    )
    params = (
        flat_first.reshape(nelem, width, hidden_width),
        flat_second.reshape(nelem, hidden_width, hidden_width),
        vectors,
    )
    positions = jnp.arange(atoms, dtype=jnp.int32)
    live = (positions[None, None, :] < counts[:, :, None]).astype(jnp.float32)

    def forward(block):
        number = block.shape[1]

        def energy_fn(weights, pieces):
            flat = pieces.reshape(nelem, number * atoms, width)
            return element_energies(weights[0], weights[1], weights[2], flat).reshape(
                nelem, number, atoms
            )

        return jax.vjp(energy_fn, params, block)

    raw, pull = forward(descriptors)
    potential_part, adjoint = structure_terms(raw * live, live, struct_ids, ref_energy)
    grads, force_partials = pull(adjoint)
    grad_first = grads[0].reshape(nelem, width * hidden_width)
    grad_second = grads[1].reshape(nelem, hidden_width * hidden_width)
    sum_first, sum_second, grad_vectors, potential_sum = lax.psum(
        (grad_first, grad_second, grads[2], potential_part), ("dp", "rep")
    )
    position = lax.axis_index(("dp", "rep"))
    share_first = lax.dynamic_slice_in_dim(
        sum_first, position * first_layer.shape[1], first_layer.shape[1], 1
    )
    share_second = lax.dynamic_slice_in_dim(
        sum_second, position * second_layer.shape[1], second_layer.shape[1], 1
    )
    new_first_mom = first_momentum - STEP_SIZE * share_first
    new_second_mom = second_momentum - STEP_SIZE * share_second
    new_vector_mom = vector_momentum - STEP_SIZE * grad_vectors
    new_first = first_layer + STEP_SIZE * new_first_mom
    new_second = second_layer + STEP_SIZE * new_second_mom
    new_vectors = vectors + STEP_SIZE * new_vector_mom
    potential = (potential_sum / (ref_energy.shape[0] * lax.axis_size(("dp", "rep")))).reshape(1)
    return (
        new_first,
        new_second,
        new_vectors,
        new_first_mom,
        new_second_mom,
        new_vector_mom,
        potential,
        force_partials,
    )


def solution(mesh):
    placed = (
        P(None, ("dp", "rep"), None, None),
        P(None, ("dp", "rep")),
        P(None, ("dp", "rep"), None),
        P(("dp", "rep")),
        P("chain", ("dp", "rep")),
        P("chain", ("dp", "rep")),
        P("chain", None, None),
        P("chain", ("dp", "rep")),
        P("chain", ("dp", "rep")),
        P("chain", None, None),
    )
    split_by_half = (mesh.shape["chain"], mesh.shape["dp"], mesh.shape["rep"]) == (2, 8, 2)
    return jax.shard_map(
        halves if split_by_half else on_device,
        mesh=mesh,
        in_specs=placed,
        out_specs=(
            P("chain", ("dp", "rep")),
            P("chain", ("dp", "rep")),
            P("chain", None, None),
            P("chain", ("dp", "rep")),
            P("chain", ("dp", "rep")),
            P("chain", None, None),
            P("chain"),
            P("chain", ("dp", "rep"), None, None),
        ),
        check_vma=False,
    )
```

```python
import jax
import jax.numpy as jnp
from jax import lax
from jax.experimental import pallas as pl
from jax.experimental.pallas import tpu as pltpu
from jax.sharding import PartitionSpec as P

NOISE_VAR = 0.1
STEP_SIZE = 0.01
HIGH = lax.Precision.HIGHEST
F32 = jnp.float32
BF16 = jnp.bfloat16
VMEM = pltpu.VMEM
LIMIT = 32 * 1024 * 1024

NT = (((1,), (1,)), ((), ()))
TN = (((0,), (0,)), ((), ()))
NN = (((1,), (0,)), ((), ()))


def split(x):
    high = x.astype(BF16)
    return high, (x - high.astype(F32)).astype(BF16)


def product(left, right, dims):
    one = lambda a, b: lax.dot_general(a, b, dims, preferred_element_type=F32)
    return one(left[0], right[0]) + (one(left[0], right[1]) + one(left[1], right[0]))


def call(kernel, outs, args, scratch=(), flops=0, size=0, name=None):
    return pl.pallas_call(
        kernel,
        out_shape=[jax.ShapeDtypeStruct(shape, kind) for shape, kind in ((*out, F32)[:2] for out in outs)],
        in_specs=[pl.BlockSpec(memory_space=VMEM)] * len(args),
        out_specs=[pl.BlockSpec(memory_space=VMEM)] * len(outs),
        scratch_shapes=list(scratch),
        compiler_params=pltpu.CompilerParams(vmem_limit_bytes=LIMIT),
        cost_estimate=pl.CostEstimate(flops=1, bytes_accessed=1, transcendentals=0),
        name=name,
    )(*args)


def place():
    spot = lax.axis_index("dp")
    return spot, lax.axis_index("rep"), spot // 4, lax.axis_index("chain")


def forward_kernel(
    desc_ref, meta_ref, first_far, second_far, far_meta, vec_ref,
    own0, own1, rec0, rec1,
    h1_ref, h2_ref, x_ref, member_ref, sums_ref, w1h, w1l, w2h, w2l,
):
    spot, core, half, chain = place()
    width = w1h.shape[1]
    rows1 = w1h.shape[0] // 16
    rows2 = w2h.shape[0] // 16
    rows = rows1 + rows2
    for far in range(2):
        for other in range(2):
            block = ((own0, own1), (rec0, rec1))[far][other]
            for delta in range(4):
                owner = ((spot ^ (delta + 4 * far)) * 2 + (core ^ other))
                piece = block[delta * rows : delta * rows + rows1, :]
                high, low = split(piece)
                at = pl.ds(pl.multiple_of(owner * rows1, rows1), rows1)
                w1h[at, :] = high
                w1l[at, :] = low
                piece = block[delta * rows + rows1 : (delta + 1) * rows, :]
                high, low = split(piece)
                at = pl.ds(pl.multiple_of(owner * rows2, rows2), rows2)
                w2h[at, :] = high
                w2l[at, :] = low
    atoms = desc_ref.shape[2]
    near = meta_ref[...]
    away = far_meta[...]
    n_near = [near[1:2, 0:1], near[1:2, 1:2]]
    n_far = [away[1:2, 0:1], away[1:2, 1:2]]
    choose = lambda number, yes, no: jnp.where(jnp.broadcast_to(number, yes.shape) > 0.5, yes, no)
    own_desc = [desc_ref[half, 0], desc_ref[half, 1]]
    direct = first_far[...]
    shared = second_far[...]
    even = chain == 0
    far_desc = [jnp.where(even, direct, shared), jnp.where(even, shared, direct)]
    first = lambda own, far: choose(n_near[0], own[0], far[0])
    second = lambda own, far: choose(n_near[1], own[1], choose(n_near[0], far[0], far[1]))
    x0, x1 = first(own_desc, far_desc), second(own_desc, far_desc)
    n0, n1 = first(n_near, n_far), second(n_near, n_far)
    near_ids = near[0:1, :]
    far_ids = away[0:1, :] + 32.0
    pair = lambda row: [row[:, :atoms], row[:, atoms:]]
    id0, id1 = first(pair(near_ids), pair(far_ids)), second(pair(near_ids), pair(far_ids))
    ids = jnp.broadcast_to(jnp.concatenate([id0, id1], axis=1), (128, 2 * atoms)).T[:, 0:128]
    spots = lax.broadcasted_iota(jnp.int32, (atoms, 128), 0).astype(F32)
    live = jnp.concatenate([(spots < n0).astype(F32), (spots < n1).astype(F32)], axis=0)
    lanes = lax.broadcasted_iota(jnp.int32, (2 * atoms, 128), 1).astype(F32)
    member = jnp.where(ids == lanes, live, 0.0)
    member_ref[...] = member

    x = jnp.concatenate([x0, x1], axis=0)
    x_ref[...] = x
    c1, c2, w3 = [vec_ref[kind, pl.ds(half, 1), :] for kind in range(3)]
    w1 = (w1h[...], w1l[...])
    w2 = (w2h[...], w2l[...])
    h1 = jnp.tanh(product(split(x), w1, NN) + c1)
    h1_ref[...] = h1
    h2 = jnp.tanh(product(split(h1), w2, NN) + c2)
    h2_ref[...] = h2
    energy = jnp.sum(h2 * w3, axis=1, keepdims=True)
    sums_ref[0:1, :] = jnp.sum(member * energy, axis=0, keepdims=True)
    sums_ref[1:2, :] = jnp.sum(member, axis=0, keepdims=True)
    sums_ref[2:8, :] = jnp.zeros((6, 128), F32)


def backward_kernel(h1_ref, h2_ref, vec_ref, w1h, w1l, w2h, w2l, g2_ref, g1_ref, f_ref):
    spot, core, half, chain = place()
    w3 = vec_ref[2, pl.ds(half, 1), :]
    h1, h2 = h1_ref[...], h2_ref[...]
    g2 = w3 * (1.0 - h2 * h2)
    g2_ref[...] = g2
    g1 = product(split(g2), (w2h[...], w2l[...]), NT) * (1.0 - h1 * h1)
    g1_ref[...] = g1
    f_ref[...] = product(split(g1), (w1h[...], w1l[...]), NT)


def force_kernel(mine, theirs, refs, near, member, f_ref, force_near, force_far, adj_ref, pot_ref):
    other = theirs[...]
    lane = lax.broadcasted_iota(jnp.int32, other.shape, 1)
    other = jnp.where(lane < 32, pltpu.roll(other, 96, 1), pltpu.roll(other, 32, 1))
    total = mine[0:1, :] + other[0:1, :]
    count = jnp.maximum(mine[1:2, :] + other[1:2, :], 1.0)
    error = total / count - refs[0:1, :]
    inside = lax.broadcasted_iota(jnp.int32, (1, 128), 1) < 64
    error = jnp.where(inside, error, 0.0)
    square = error * error
    low = jnp.sum(square[:, 0:32], axis=1, keepdims=True)
    high = jnp.sum(square[:, 32:64], axis=1, keepdims=True)
    pot_ref[...] = jnp.broadcast_to((low + high) / (2.0 * NOISE_VAR), (8, 128))
    scale = error / count / NOISE_VAR
    adj = jnp.sum(member[...] * scale, axis=1, keepdims=True)
    adj_ref[...] = jnp.broadcast_to(adj, adj_ref.shape)
    force = adj * f_ref[...]
    atoms = force.shape[0] // 2
    f0, f1 = force[:atoms], force[atoms:]
    has0 = jnp.broadcast_to(near[1:2, 0:1], f0.shape) > 0.5
    has1 = jnp.broadcast_to(near[1:2, 1:2], f0.shape) > 0.5
    force_near[0] = jnp.where(has0, f0, 0.0)
    force_near[1] = jnp.where(has1, f1, 0.0)
    force_far[0] = jnp.where(has0, jnp.where(has1, 0.0, f1), f0)
    force_far[1] = jnp.where(has0, 0.0, f1)


def gradient_kernel(
    adj_ref, pot_ref, h1_ref, h2_ref, g2_ref, g1_ref, x_ref, keep_far, give_far, keep_near, give_near, dw1, dw2,
):
    spot, core, half, chain = place()
    adj = adj_ref[...][:, 0:1]
    g2 = adj * g2_ref[...]
    g1 = adj * g1_ref[...]
    dw2[...] = product(split(h1_ref[...]), split(g2), TN)
    dw1[...] = product(split(x_ref[...]), split(g1), TN)
    rows1 = dw1.shape[0] // 16
    rows2 = dw2.shape[0] // 16
    rows = rows1 + rows2
    for far, keep, give in ((4, keep_far, give_far), (0, keep_near, give_near)):
        for index, delta in enumerate((0, 2, 1, 3)):
            for out, holder in ((keep, core), (give, 1 - core)):
                owner = (spot ^ (delta + far)) * 2 + holder
                base = index * rows
                at = pl.ds(pl.multiple_of(owner * rows1, rows1), rows1)
                out[base : base + rows1, :] = dw1[at, :]
                at = pl.ds(pl.multiple_of(owner * rows2, rows2), rows2)
                out[base + rows1 : base + rows, :] = dw2[at, :]
    base = 4 * rows
    width = g2.shape[1]
    vec = [
        jnp.sum(g1, axis=0, keepdims=True),
        jnp.sum(g2, axis=0, keepdims=True),
        jnp.sum(adj * h2_ref[...], axis=0, keepdims=True),
        jnp.broadcast_to(pot_ref[0:1, 0:1], (1, width)),
    ]
    tail = jnp.concatenate(vec + [jnp.zeros((4, width), F32)], axis=0)
    keep_far[base : base + 8, :] = tail
    give_far[base : base + 8, :] = tail


def halving_kernel(keep, came, stay, leave):
    tail = stay.shape[0] % 48
    rows = stay.shape[0] - tail
    stay[0:rows, :] = keep[0:rows, :] + came[0:rows, :]
    leave[0:rows, :] = keep[rows : 2 * rows, :] + came[rows : 2 * rows, :]
    if tail:
        end = keep[2 * rows :, :] + came[2 * rows :, :]
        stay[rows:, :] = end
        leave[rows:, :] = end


def sum_kernel(a, b, *rest):
    out = rest[-1]
    out[...] = a[...] + b[...]


def message_kernel(desc_hbm, counts_hbm, ids_hbm, refs_hbm, message, near, counts, ids, refs, sems):
    spot, core, half, chain = place()
    atoms = message.shape[0] - 8
    loads = [
        pltpu.make_async_copy(source, target, sems.at[index])
        for index, (source, target) in enumerate(
            (
                (counts_hbm, counts),
                (ids_hbm, ids),
                (refs_hbm, refs),
                (desc_hbm.at[1 - half, chain], message.at[pl.ds(0, atoms)]),
            )
        )
    ]
    for load in loads:
        load.start()
    for load in loads:
        load.wait()
    for out, base, element in ((near, 0, half), (message, atoms, 1 - half)):
        out[base : base + 8, :] = jnp.zeros((8, 2 * atoms), F32)
        row = ids[element].astype(F32)
        out[base : base + 1, 0:atoms] = row[0:1]
        out[base : base + 1, atoms:] = row[1:2]
        number = counts[pl.ds(element, 1), :].astype(F32)
        out[base + 1 : base + 2, 0:2] = number
        out[base + 2 : base + 3, 0 : refs.shape[1]] = refs[...]


def near_kernel(a, b, force_near, force_came, mine_first, mine_second, forces, total, sems):
    spot, core, half, chain = place()
    near_copy = pltpu.make_async_copy(force_near, forces.at[half], sems.at[0])
    far_copy = pltpu.make_async_copy(force_came, forces.at[1 - half], sems.at[1])
    near_copy.start()
    far_copy.start()
    total[...] = a[...] + b[...]
    hidden = total.shape[1]
    rows1 = mine_first.shape[1] // hidden
    rows2 = mine_second.shape[1] // hidden
    for row in range(rows1):
        mine_first[:, row * hidden : (row + 1) * hidden] = total[row : row + 1, :]
    for row in range(rows2):
        mine_second[:, row * hidden : (row + 1) * hidden] = total[rows1 + row : rows1 + row + 1, :]
    near_copy.wait()
    far_copy.wait()


def final_kernel(
    mine_first, mine_second, beyond, came, first, second, vec, first_mom, second_mom, vec_mom,
    new_first, new_second, new_vec, new_first_mom, new_second_mom, new_vec_mom, potential,
    flat_first, flat_second,
):
    spot, core, half, chain = place()
    hidden = came.shape[1]
    rows1 = flat_first.shape[1] // hidden
    rows2 = flat_second.shape[1] // hidden
    rows = rows1 + rows2
    flat_first[pl.ds(half, 1), :] = mine_first[...]
    flat_second[pl.ds(half, 1), :] = mine_second[...]
    for row in range(rows1):
        flat_first[pl.ds(1 - half, 1), row * hidden : (row + 1) * hidden] = came[row : row + 1, :]
    for row in range(rows2):
        flat_second[pl.ds(1 - half, 1), row * hidden : (row + 1) * hidden] = came[rows1 + row : rows1 + row + 1, :]
    for grad, value, momentum, new_value, new_momentum in (
        (flat_first, first, first_mom, new_first, new_first_mom),
        (flat_second, second, second_mom, new_second, new_second_mom),
    ):
        moved = momentum[...] - STEP_SIZE * grad[...]
        new_momentum[...] = moved
        new_value[...] = value[...] + STEP_SIZE * moved
    low = jnp.full((1, hidden), half, jnp.int32) == 0
    for kind in range(3):
        own = beyond[rows + kind : rows + kind + 1, :]
        other = came[rows + kind : rows + kind + 1, :]
        for element in range(2):
            grad = jnp.where(low, own, other) if element == 0 else jnp.where(low, other, own)
            moved = vec_mom[kind, element : element + 1, :] - STEP_SIZE * grad
            new_vec_mom[kind, element : element + 1, :] = moved
            new_vec[kind, element : element + 1, :] = vec[kind, element : element + 1, :] + STEP_SIZE * moved
    potential[...] = beyond[rows + 3 : rows + 4, 0:128] * (1.0 / 512.0)


def after(value, *others):
    return lax.optimization_barrier((value,) + others)[0]


def flip(axis, delta, size):
    return lambda x: lax.ppermute(x, axis, [(i, i ^ delta) for i in range(size)])


def halves(
    descriptors, counts, struct_ids, ref_energy, first_layer, second_layer, vectors,
    first_momentum, second_momentum, vector_momentum,
):
    nelem, slots, atoms, width = descriptors.shape
    hidden = vectors.shape[2]
    structs = ref_energy.shape[0]
    spot, core, half, chain = place()
    to = [None] + [flip("dp", delta, 8) for delta in range(1, 8)]
    to_core = flip("rep", 1, 2)
    to_chain = flip("chain", 1, 2)
    rows1 = first_layer.shape[1] // hidden
    rows2 = second_layer.shape[1] // hidden
    rows = rows1 + rows2
    shards = jnp.concatenate(
        [first_layer.reshape(nelem, rows1, hidden), second_layer.reshape(nelem, rows2, hidden)], axis=1
    )
    pick = lambda x, at: lax.dynamic_index_in_dim(x, at, 0, keepdims=False)
    own = pick(shards, half)
    got = to[4](pick(shards, 1 - half))

    any_space = pl.BlockSpec(memory_space=pl.ANY)
    vmem = pl.BlockSpec(memory_space=VMEM)
    message, meta = pl.pallas_call(
        message_kernel,
        out_shape=[jax.ShapeDtypeStruct((atoms + 8, width), F32), jax.ShapeDtypeStruct((8, width), F32)],
        in_specs=[pl.BlockSpec(memory_space=pltpu.HBM)] * 4,
        out_specs=[vmem] * 2,
        scratch_shapes=[
            pltpu.VMEM(counts.shape, jnp.int32), pltpu.VMEM(struct_ids.shape, jnp.int32), pltpu.VMEM((1, structs), F32),
            pltpu.SemaphoreType.DMA((4,)),
        ],
        compiler_params=pltpu.CompilerParams(vmem_limit_bytes=4 * 1024 * 1024),
        name="message",
    )(descriptors, counts, struct_ids, ref_energy.reshape(1, structs))
    message = to[4](message)
    own_z = to[2](own)
    own_x = to[1](jnp.concatenate([own, own_z]))
    own_came = [own_x[:rows], own_z, own_x[rows:]]
    got = after(got, own)
    direct = message[:atoms]
    far_meta = message[atoms:]
    shared = to_chain(direct)
    own_set = jnp.concatenate(lax.optimization_barrier((own, *own_came, got))[:4], axis=0)
    own_across = to_core(own_set)
    got_z = to[2](got)
    got_x = to[1](jnp.concatenate([got, got_z]))
    got_set = jnp.concatenate([got, got_x[:rows], got_z, got_x[rows:]], axis=0)
    got_across = to_core(after(got_set, shared))

    work = slots * atoms
    vec = vectors.transpose(1, 0, 2)
    h1, h2, x, member, sums, *weights = call(
        forward_kernel,
        [((work, hidden),)] * 2 + [((work, width),), ((work, 128),), ((8, 128),)]
        + [((width, hidden), BF16)] * 2 + [((hidden, hidden), BF16)] * 2,
        (descriptors, meta, direct, shared, far_meta, vec, own_set, own_across, got_set, got_across),
        flops=6 * work * hidden * (width + hidden),
        size=6 * 1024 * 1024,
        name="forward",
    )
    sums_came = to[4](sums)
    g2, g1, f = call(
        backward_kernel,
        [((work, hidden),)] * 2 + [((work, width),)],
        (h1, h2, vec, *weights),
        flops=6 * work * hidden * (width + hidden),
        size=6 * 1024 * 1024,
        name="backward",
    )
    refs = jnp.concatenate([meta[2:3, 0:structs], far_meta[2:3, 0:structs], jnp.zeros((1, 128 - 2 * structs), F32)], axis=1)
    force_near, force_far, adj, pot = call(
        force_kernel,
        [((slots, atoms, width),)] * 2 + [((work, 128),), ((8, 128),)],
        (sums, sums_came, refs, meta, member, f),
        size=2 * 1024 * 1024,
        name="force",
    )
    force_came = to[4](force_far)
    tail = 8
    group = 4 * rows
    keep_far, give_far, keep_near, give_near = call(
        gradient_kernel,
        [((group + tail, hidden),)] * 2 + [((group, hidden),)] * 2,
        (adj, pot, h1, h2, g2, g1, x),
        scratch=[pltpu.VMEM((width, hidden), F32), pltpu.VMEM((hidden, hidden), F32)],
        flops=6 * work * hidden * (width + hidden),
        size=4 * 1024 * 1024,
        name="gradient",
    )

    def halve(keep, came, end, name):
        left = (keep.shape[0] - end) // 2 + end
        return call(halving_kernel, [((left, hidden),)] * 2, (keep, came), size=4 * 4 * left * hidden, name=name)

    far_stay, far_leave = halve(keep_far, to_core(give_far), tail, "far_core")
    near_stay, near_leave = halve(keep_near, to_core(give_near), 0, "near_core")
    far_came = to[1](far_leave)
    far_stay, far_leave = halve(far_stay, far_came, tail, "far_x")
    near_came = to[1](after(near_leave, far_came))
    far_came = to[2](far_leave)
    near_stay, near_leave = halve(near_stay, near_came, 0, "near_x")
    token = force_came[0, 0:8, 0:128]
    token = to_core(token)
    (beyond_sum,) = call(sum_kernel, [((rows + tail, hidden),)], (far_stay, far_came, token), name="far_z")
    came = to[4](beyond_sum)
    last_came = to[2](near_leave)
    shape = lambda x: jax.ShapeDtypeStruct(x.shape, F32)
    vec_mom = vector_momentum.transpose(1, 0, 2)
    mine_first, mine_second, force_partials = pl.pallas_call(
        near_kernel,
        out_shape=[
            jax.ShapeDtypeStruct((1, first_layer.shape[1]), F32), jax.ShapeDtypeStruct((1, second_layer.shape[1]), F32),
            shape(descriptors),
        ],
        in_specs=[vmem] * 4,
        out_specs=[vmem] * 2 + [any_space],
        scratch_shapes=[pltpu.VMEM((rows, hidden), F32), pltpu.SemaphoreType.DMA((2,))],
        compiler_params=pltpu.CompilerParams(vmem_limit_bytes=8 * 1024 * 1024),
        cost_estimate=pl.CostEstimate(flops=1, bytes_accessed=1, transcendentals=0),
        name="near_z",
    )(near_stay, last_came, force_near, force_came)
    (
        new_first, new_second, new_vec, new_first_mom, new_second_mom, new_vec_mom, potential,
    ) = pl.pallas_call(
        final_kernel,
        out_shape=[
            shape(first_layer), shape(second_layer), shape(vec), shape(first_layer), shape(second_layer), shape(vec),
            jax.ShapeDtypeStruct((1, 128), F32),
        ],
        in_specs=[vmem] * 10,
        out_specs=[vmem] * 7,
        scratch_shapes=[pltpu.VMEM(first_layer.shape, F32), pltpu.VMEM(second_layer.shape, F32)],
        compiler_params=pltpu.CompilerParams(vmem_limit_bytes=8 * 1024 * 1024),
        cost_estimate=pl.CostEstimate(flops=1, bytes_accessed=1, transcendentals=0),
        name="final",
    )(
        mine_first, mine_second, beyond_sum, came, first_layer, second_layer, vec, first_momentum, second_momentum, vec_mom,
    )
    return (
        new_first, new_second, new_vec.transpose(1, 0, 2), new_first_mom, new_second_mom,
        new_vec_mom.transpose(1, 0, 2), potential[0, 0:1], force_partials,
    )


def element_energies(first, second, vectors, desc):
    lower = jnp.einsum("erf,efj->erj", desc, first, precision=HIGH) + vectors[:, 0][:, None, :]
    hidden = jnp.tanh(lower)
    upper = jnp.einsum("erj,ejk->erk", hidden, second, precision=HIGH) + vectors[:, 1][:, None, :]
    top = jnp.tanh(upper)
    return jnp.einsum("erk,ek->er", top, vectors[:, 2], precision=HIGH)


def structure_terms(energies, live, ids, refs):
    member = (
        ids[..., None] == jnp.arange(refs.shape[0], dtype=jnp.int32)[None, None, None, :]
    ).astype(jnp.float32)
    total = jnp.einsum("ebas,eba->s", member, energies, precision=HIGH)
    count = jnp.maximum(jnp.einsum("ebas,eba->s", member, live, precision=HIGH), 1.0)
    error = total / count - refs
    potential_part = jnp.sum(error * error) / (2.0 * NOISE_VAR)
    scale = error / count / NOISE_VAR
    adjoint = jnp.einsum("ebas,s->eba", member, scale, precision=HIGH) * live
    return (potential_part, adjoint)


def on_device(
    descriptors,
    counts,
    struct_ids,
    ref_energy,
    first_layer,
    second_layer,
    vectors,
    first_momentum,
    second_momentum,
    vector_momentum,
):
    nelem, slots, atoms, width = descriptors.shape
    hidden_width = vectors.shape[2]
    flat_first, flat_second = (
        lax.all_gather(first_layer, ("dp", "rep"), axis=1, tiled=True),
        lax.all_gather(second_layer, ("dp", "rep"), axis=1, tiled=True),
    )
    params = (
        flat_first.reshape(nelem, width, hidden_width),
        flat_second.reshape(nelem, hidden_width, hidden_width),
        vectors,
    )
    positions = jnp.arange(atoms, dtype=jnp.int32)
    live = (positions[None, None, :] < counts[:, :, None]).astype(jnp.float32)

    def forward(block):
        number = block.shape[1]

        def energy_fn(weights, pieces):
            flat = pieces.reshape(nelem, number * atoms, width)
            return element_energies(weights[0], weights[1], weights[2], flat).reshape(
                nelem, number, atoms
            )

        return jax.vjp(energy_fn, params, block)

    raw, pull = forward(descriptors)
    potential_part, adjoint = structure_terms(raw * live, live, struct_ids, ref_energy)
    grads, force_partials = pull(adjoint)
    grad_first = grads[0].reshape(nelem, width * hidden_width)
    grad_second = grads[1].reshape(nelem, hidden_width * hidden_width)
    sum_first, sum_second, grad_vectors, potential_sum = lax.psum(
        (grad_first, grad_second, grads[2], potential_part), ("dp", "rep")
    )
    position = lax.axis_index(("dp", "rep"))
    share_first = lax.dynamic_slice_in_dim(
        sum_first, position * first_layer.shape[1], first_layer.shape[1], 1
    )
    share_second = lax.dynamic_slice_in_dim(
        sum_second, position * second_layer.shape[1], second_layer.shape[1], 1
    )
    new_first_mom = first_momentum - STEP_SIZE * share_first
    new_second_mom = second_momentum - STEP_SIZE * share_second
    new_vector_mom = vector_momentum - STEP_SIZE * grad_vectors
    new_first = first_layer + STEP_SIZE * new_first_mom
    new_second = second_layer + STEP_SIZE * new_second_mom
    new_vectors = vectors + STEP_SIZE * new_vector_mom
    potential = (potential_sum / (ref_energy.shape[0] * lax.axis_size(("dp", "rep")))).reshape(1)
    return (
        new_first,
        new_second,
        new_vectors,
        new_first_mom,
        new_second_mom,
        new_vector_mom,
        potential,
        force_partials,
    )


def solution(mesh):
    placed = (
        P(None, ("dp", "rep"), None, None),
        P(None, ("dp", "rep")),
        P(None, ("dp", "rep"), None),
        P(("dp", "rep")),
        P("chain", ("dp", "rep")),
        P("chain", ("dp", "rep")),
        P("chain", None, None),
        P("chain", ("dp", "rep")),
        P("chain", ("dp", "rep")),
        P("chain", None, None),
    )
    split_by_half = (mesh.shape["chain"], mesh.shape["dp"], mesh.shape["rep"]) == (2, 8, 2)
    return jax.shard_map(
        halves if split_by_half else on_device,
        mesh=mesh,
        in_specs=placed,
        out_specs=(
            P("chain", ("dp", "rep")),
            P("chain", ("dp", "rep")),
            P("chain", None, None),
            P("chain", ("dp", "rep")),
            P("chain", ("dp", "rep")),
            P("chain", None, None),
            P("chain"),
            P("chain", ("dp", "rep"), None, None),
        ),
        check_vma=False,
    )
```

```python
import jax
import jax.numpy as jnp
from jax import lax
from jax.experimental import pallas as pl
from jax.experimental.pallas import tpu as pltpu
from jax.sharding import PartitionSpec as P

NOISE_VAR = 0.1
STEP_SIZE = 0.01
HIGH = lax.Precision.HIGHEST
F32 = jnp.float32
BF16 = jnp.bfloat16
VMEM = pltpu.VMEM
LIMIT = 32 * 1024 * 1024

NT = (((1,), (1,)), ((), ()))
TN = (((0,), (0,)), ((), ()))
NN = (((1,), (0,)), ((), ()))


def split(x):
    high = x.astype(BF16)
    return high, (x - high.astype(F32)).astype(BF16)


def product(left, right, dims):
    one = lambda a, b: lax.dot_general(a, b, dims, preferred_element_type=F32)
    return one(left[0], right[0]) + (one(left[0], right[1]) + one(left[1], right[0]))


def call(kernel, outs, args, scratch=(), flops=0, size=0, name=None):
    return pl.pallas_call(
        kernel,
        out_shape=[jax.ShapeDtypeStruct(shape, kind) for shape, kind in ((*out, F32)[:2] for out in outs)],
        in_specs=[pl.BlockSpec(memory_space=VMEM)] * len(args),
        out_specs=[pl.BlockSpec(memory_space=VMEM)] * len(outs),
        scratch_shapes=list(scratch),
        compiler_params=pltpu.CompilerParams(vmem_limit_bytes=LIMIT),
        cost_estimate=pl.CostEstimate(flops=1, bytes_accessed=1, transcendentals=0),
        name=name,
    )(*args)


def place():
    spot = lax.axis_index("dp")
    return spot, lax.axis_index("rep"), spot // 4, lax.axis_index("chain")


def forward_kernel(
    desc_ref, meta_ref, first_far, second_far, far_meta, vec_ref,
    own0, own1, rec0, rec1,
    h1_ref, h2_ref, x_ref, member_ref, sums_ref, w1h, w1l, w2h, w2l,
):
    spot, core, half, chain = place()
    width = w1h.shape[1]
    rows1 = w1h.shape[0] // 16
    rows2 = w2h.shape[0] // 16
    rows = rows1 + rows2
    for far in range(2):
        for other in range(2):
            block = ((own0, own1), (rec0, rec1))[far][other]
            for delta in range(4):
                owner = ((spot ^ (delta + 4 * far)) * 2 + (core ^ other))
                piece = block[delta * rows : delta * rows + rows1, :]
                high, low = split(piece)
                at = pl.ds(pl.multiple_of(owner * rows1, rows1), rows1)
                w1h[at, :] = high
                w1l[at, :] = low
                piece = block[delta * rows + rows1 : (delta + 1) * rows, :]
                high, low = split(piece)
                at = pl.ds(pl.multiple_of(owner * rows2, rows2), rows2)
                w2h[at, :] = high
                w2l[at, :] = low
    atoms = desc_ref.shape[2]
    near = meta_ref[...]
    away = far_meta[...]
    n_near = [near[1:2, 0:1], near[1:2, 1:2]]
    n_far = [away[1:2, 0:1], away[1:2, 1:2]]
    choose = lambda number, yes, no: jnp.where(jnp.broadcast_to(number, yes.shape) > 0.5, yes, no)
    own_desc = [desc_ref[half, 0], desc_ref[half, 1]]
    direct = first_far[...]
    shared = second_far[...]
    even = chain == 0
    far_desc = [jnp.where(even, direct, shared), jnp.where(even, shared, direct)]
    first = lambda own, far: choose(n_near[0], own[0], far[0])
    second = lambda own, far: choose(n_near[1], own[1], choose(n_near[0], far[0], far[1]))
    x0, x1 = first(own_desc, far_desc), second(own_desc, far_desc)
    n0, n1 = first(n_near, n_far), second(n_near, n_far)
    near_ids = near[0:1, :]
    far_ids = away[0:1, :] + 32.0
    pair = lambda row: [row[:, :atoms], row[:, atoms:]]
    id0, id1 = first(pair(near_ids), pair(far_ids)), second(pair(near_ids), pair(far_ids))
    ids = jnp.broadcast_to(jnp.concatenate([id0, id1], axis=1), (128, 2 * atoms)).T[:, 0:128]
    spots = lax.broadcasted_iota(jnp.int32, (atoms, 128), 0).astype(F32)
    live = jnp.concatenate([(spots < n0).astype(F32), (spots < n1).astype(F32)], axis=0)
    lanes = lax.broadcasted_iota(jnp.int32, (2 * atoms, 128), 1).astype(F32)
    member = jnp.where(ids == lanes, live, 0.0)
    member_ref[...] = member

    x = jnp.concatenate([x0, x1], axis=0)
    x_ref[...] = x
    c1, c2, w3 = [vec_ref[kind, pl.ds(half, 1), :] for kind in range(3)]
    w1 = (w1h[...], w1l[...])
    w2 = (w2h[...], w2l[...])
    h1 = jnp.tanh(product(split(x), w1, NN) + c1)
    h1_ref[...] = h1
    h2 = jnp.tanh(product(split(h1), w2, NN) + c2)
    h2_ref[...] = h2
    energy = jnp.sum(h2 * w3, axis=1, keepdims=True)
    sums_ref[0:1, :] = jnp.sum(member * energy, axis=0, keepdims=True)
    sums_ref[1:2, :] = jnp.sum(member, axis=0, keepdims=True)
    sums_ref[2:8, :] = jnp.zeros((6, 128), F32)


def backward_kernel(h1_ref, h2_ref, vec_ref, w1h, w1l, w2h, w2l, g2_ref, g1_ref, f_ref):
    spot, core, half, chain = place()
    w3 = vec_ref[2, pl.ds(half, 1), :]
    h1, h2 = h1_ref[...], h2_ref[...]
    g2 = w3 * (1.0 - h2 * h2)
    g2_ref[...] = g2
    g1 = product(split(g2), (w2h[...], w2l[...]), NT) * (1.0 - h1 * h1)
    g1_ref[...] = g1
    f_ref[...] = product(split(g1), (w1h[...], w1l[...]), NT)


def force_kernel(mine, theirs, refs, near, member, f_ref, force_near, force_far, adj_ref, pot_ref):
    other = theirs[...]
    lane = lax.broadcasted_iota(jnp.int32, other.shape, 1)
    other = jnp.where(lane < 32, pltpu.roll(other, 96, 1), pltpu.roll(other, 32, 1))
    total = mine[0:1, :] + other[0:1, :]
    count = jnp.maximum(mine[1:2, :] + other[1:2, :], 1.0)
    error = total / count - refs[0:1, :]
    inside = lax.broadcasted_iota(jnp.int32, (1, 128), 1) < 64
    error = jnp.where(inside, error, 0.0)
    square = error * error
    low = jnp.sum(square[:, 0:32], axis=1, keepdims=True)
    high = jnp.sum(square[:, 32:64], axis=1, keepdims=True)
    pot_ref[...] = jnp.broadcast_to((low + high) / (2.0 * NOISE_VAR), (8, 128))
    scale = error / count / NOISE_VAR
    adj = jnp.sum(member[...] * scale, axis=1, keepdims=True)
    adj_ref[...] = jnp.broadcast_to(adj, adj_ref.shape)
    force = adj * f_ref[...]
    atoms = force.shape[0] // 2
    f0, f1 = force[:atoms], force[atoms:]
    has0 = jnp.broadcast_to(near[1:2, 0:1], f0.shape) > 0.5
    has1 = jnp.broadcast_to(near[1:2, 1:2], f0.shape) > 0.5
    force_near[0] = jnp.where(has0, f0, 0.0)
    force_near[1] = jnp.where(has1, f1, 0.0)
    force_far[0] = jnp.where(has0, jnp.where(has1, 0.0, f1), f0)
    force_far[1] = jnp.where(has0, 0.0, f1)


def gradient_kernel(
    adj_ref, pot_ref, h1_ref, h2_ref, g2_ref, g1_ref, x_ref, keep_all, give_all, dw1, dw2,
):
    spot, core, half, chain = place()
    adj = adj_ref[...][:, 0:1]
    g2 = adj * g2_ref[...]
    g1 = adj * g1_ref[...]
    dw2[...] = product(split(h1_ref[...]), split(g2), TN)
    dw1[...] = product(split(x_ref[...]), split(g1), TN)
    rows1 = dw1.shape[0] // 16
    rows2 = dw2.shape[0] // 16
    rows = rows1 + rows2
    middle = 4 * rows + 8
    keep_far, give_far = [ref.at[pl.ds(0, middle)] for ref in (keep_all, give_all)]
    keep_near, give_near = [ref.at[pl.ds(middle, 4 * rows)] for ref in (keep_all, give_all)]
    for far, keep, give in ((4, keep_far, give_far), (0, keep_near, give_near)):
        for index, delta in enumerate((0, 2, 1, 3)):
            for out, holder in ((keep, core), (give, 1 - core)):
                owner = (spot ^ (delta + far)) * 2 + holder
                base = index * rows
                at = pl.ds(pl.multiple_of(owner * rows1, rows1), rows1)
                out[base : base + rows1, :] = dw1[at, :]
                at = pl.ds(pl.multiple_of(owner * rows2, rows2), rows2)
                out[base + rows1 : base + rows, :] = dw2[at, :]
    base = 4 * rows
    width = g2.shape[1]
    vec = [
        jnp.sum(g1, axis=0, keepdims=True),
        jnp.sum(g2, axis=0, keepdims=True),
        jnp.sum(adj * h2_ref[...], axis=0, keepdims=True),
        jnp.broadcast_to(pot_ref[0:1, 0:1], (1, width)),
    ]
    tail = jnp.concatenate(vec + [jnp.zeros((4, width), F32)], axis=0)
    keep_far[base : base + 8, :] = tail
    give_far[base : base + 8, :] = tail


def halving_kernel(keep, came, stay, leave):
    tail = stay.shape[0] % 48
    rows = stay.shape[0] - tail
    stay[0:rows, :] = keep[0:rows, :] + came[0:rows, :]
    leave[0:rows, :] = keep[rows : 2 * rows, :] + came[rows : 2 * rows, :]
    if tail:
        end = keep[2 * rows :, :] + came[2 * rows :, :]
        stay[rows:, :] = end
        leave[rows:, :] = end


def core_kernel(keep, came, far_stay, far_leave, near_stay, near_leave):
    half_rows = near_stay.shape[0]
    tail = far_stay.shape[0] - half_rows
    far_rows = 2 * half_rows + tail
    total = lambda start, rows: keep[start : start + rows, :] + came[start : start + rows, :]
    far_stay[0:half_rows, :] = total(0, half_rows)
    far_leave[0:half_rows, :] = total(half_rows, half_rows)
    end = total(2 * half_rows, tail)
    far_stay[half_rows:, :] = end
    far_leave[half_rows:, :] = end
    near_stay[...] = total(far_rows, half_rows)
    near_leave[...] = total(far_rows + half_rows, half_rows)


def sum_kernel(a, b, *rest):
    out = rest[-1]
    out[...] = a[...] + b[...]


def message_kernel(desc_hbm, counts_hbm, ids_hbm, refs_hbm, message, near, counts, ids, refs, sems):
    spot, core, half, chain = place()
    atoms = message.shape[0] - 8
    loads = [
        pltpu.make_async_copy(source, target, sems.at[index])
        for index, (source, target) in enumerate(
            (
                (counts_hbm, counts),
                (ids_hbm, ids),
                (refs_hbm, refs),
                (desc_hbm.at[1 - half, chain], message.at[pl.ds(0, atoms)]),
            )
        )
    ]
    for load in loads:
        load.start()
    for load in loads:
        load.wait()
    for out, base, element in ((near, 0, half), (message, atoms, 1 - half)):
        out[base : base + 8, :] = jnp.zeros((8, 2 * atoms), F32)
        row = ids[element].astype(F32)
        out[base : base + 1, 0:atoms] = row[0:1]
        out[base : base + 1, atoms:] = row[1:2]
        number = counts[pl.ds(element, 1), :].astype(F32)
        out[base + 1 : base + 2, 0:2] = number
        out[base + 2 : base + 3, 0 : refs.shape[1]] = refs[...]


def near_kernel(a, b, force_near, force_came, mine_first, mine_second, forces, total, sems):
    spot, core, half, chain = place()
    near_copy = pltpu.make_async_copy(force_near, forces.at[half], sems.at[0])
    far_copy = pltpu.make_async_copy(force_came, forces.at[1 - half], sems.at[1])
    near_copy.start()
    far_copy.start()
    total[...] = a[...] + b[...]
    hidden = total.shape[1]
    rows1 = mine_first.shape[1] // hidden
    rows2 = mine_second.shape[1] // hidden
    for row in range(rows1):
        mine_first[:, row * hidden : (row + 1) * hidden] = total[row : row + 1, :]
    for row in range(rows2):
        mine_second[:, row * hidden : (row + 1) * hidden] = total[rows1 + row : rows1 + row + 1, :]
    near_copy.wait()
    far_copy.wait()


def final_kernel(
    mine_first, mine_second, beyond, came, first, second, vec, first_mom, second_mom, vec_mom,
    new_first, new_second, new_vec, new_first_mom, new_second_mom, new_vec_mom, potential,
    flat_first, flat_second,
):
    spot, core, half, chain = place()
    hidden = came.shape[1]
    rows1 = flat_first.shape[1] // hidden
    rows2 = flat_second.shape[1] // hidden
    rows = rows1 + rows2
    flat_first[pl.ds(half, 1), :] = mine_first[...]
    flat_second[pl.ds(half, 1), :] = mine_second[...]
    for row in range(rows1):
        flat_first[pl.ds(1 - half, 1), row * hidden : (row + 1) * hidden] = came[row : row + 1, :]
    for row in range(rows2):
        flat_second[pl.ds(1 - half, 1), row * hidden : (row + 1) * hidden] = came[rows1 + row : rows1 + row + 1, :]
    for grad, value, momentum, new_value, new_momentum in (
        (flat_first, first, first_mom, new_first, new_first_mom),
        (flat_second, second, second_mom, new_second, new_second_mom),
    ):
        moved = momentum[...] - STEP_SIZE * grad[...]
        new_momentum[...] = moved
        new_value[...] = value[...] + STEP_SIZE * moved
    low = jnp.full((1, hidden), half, jnp.int32) == 0
    for kind in range(3):
        own = beyond[rows + kind : rows + kind + 1, :]
        other = came[rows + kind : rows + kind + 1, :]
        for element in range(2):
            grad = jnp.where(low, own, other) if element == 0 else jnp.where(low, other, own)
            moved = vec_mom[kind, element : element + 1, :] - STEP_SIZE * grad
            new_vec_mom[kind, element : element + 1, :] = moved
            new_vec[kind, element : element + 1, :] = vec[kind, element : element + 1, :] + STEP_SIZE * moved
    potential[...] = beyond[rows + 3 : rows + 4, 0:128] * (1.0 / 512.0)


def after(value, *others):
    return lax.optimization_barrier((value,) + others)[0]


def flip(axis, delta, size):
    return lambda x: lax.ppermute(x, axis, [(i, i ^ delta) for i in range(size)])


def halves(
    descriptors, counts, struct_ids, ref_energy, first_layer, second_layer, vectors,
    first_momentum, second_momentum, vector_momentum,
):
    nelem, slots, atoms, width = descriptors.shape
    hidden = vectors.shape[2]
    structs = ref_energy.shape[0]
    spot, core, half, chain = place()
    to = [None] + [flip("dp", delta, 8) for delta in range(1, 8)]
    to_core = flip("rep", 1, 2)
    to_chain = flip("chain", 1, 2)
    rows1 = first_layer.shape[1] // hidden
    rows2 = second_layer.shape[1] // hidden
    rows = rows1 + rows2
    shards = jnp.concatenate(
        [first_layer.reshape(nelem, rows1, hidden), second_layer.reshape(nelem, rows2, hidden)], axis=1
    )
    pick = lambda x, at: lax.dynamic_index_in_dim(x, at, 0, keepdims=False)
    own = pick(shards, half)
    got = to[4](pick(shards, 1 - half))

    any_space = pl.BlockSpec(memory_space=pl.ANY)
    vmem = pl.BlockSpec(memory_space=VMEM)
    message, meta = pl.pallas_call(
        message_kernel,
        out_shape=[jax.ShapeDtypeStruct((atoms + 8, width), F32), jax.ShapeDtypeStruct((8, width), F32)],
        in_specs=[pl.BlockSpec(memory_space=pltpu.HBM)] * 4,
        out_specs=[vmem] * 2,
        scratch_shapes=[
            pltpu.VMEM(counts.shape, jnp.int32), pltpu.VMEM(struct_ids.shape, jnp.int32), pltpu.VMEM((1, structs), F32),
            pltpu.SemaphoreType.DMA((4,)),
        ],
        compiler_params=pltpu.CompilerParams(vmem_limit_bytes=4 * 1024 * 1024),
        name="message",
    )(descriptors, counts, struct_ids, ref_energy.reshape(1, structs))
    message = to[4](message)
    own_z = to[2](own)
    own_x = to[1](jnp.concatenate([own, own_z]))
    own_came = [own_x[:rows], own_z, own_x[rows:]]
    got = after(got, own)
    direct = message[:atoms]
    far_meta = message[atoms:]
    shared = to_chain(direct)
    own_set = jnp.concatenate(lax.optimization_barrier((own, *own_came, got))[:4], axis=0)
    own_across = to_core(own_set)
    got_z = to[2](got)
    got_x = to[1](jnp.concatenate([got, got_z]))
    got_set = jnp.concatenate([got, got_x[:rows], got_z, got_x[rows:]], axis=0)
    got_across = to_core(after(got_set, shared))

    work = slots * atoms
    vec = vectors.transpose(1, 0, 2)
    h1, h2, x, member, sums, *weights = call(
        forward_kernel,
        [((work, hidden),)] * 2 + [((work, width),), ((work, 128),), ((8, 128),)]
        + [((width, hidden), BF16)] * 2 + [((hidden, hidden), BF16)] * 2,
        (descriptors, meta, direct, shared, far_meta, vec, own_set, own_across, got_set, got_across),
        flops=6 * work * hidden * (width + hidden),
        size=6 * 1024 * 1024,
        name="forward",
    )
    sums_came = to[4](sums)
    g2, g1, f = call(
        backward_kernel,
        [((work, hidden),)] * 2 + [((work, width),)],
        (h1, h2, vec, *weights),
        flops=6 * work * hidden * (width + hidden),
        size=6 * 1024 * 1024,
        name="backward",
    )
    refs = jnp.concatenate([meta[2:3, 0:structs], far_meta[2:3, 0:structs], jnp.zeros((1, 128 - 2 * structs), F32)], axis=1)
    force_near, force_far, adj, pot = call(
        force_kernel,
        [((slots, atoms, width),)] * 2 + [((work, 128),), ((8, 128),)],
        (sums, sums_came, refs, meta, member, f),
        size=2 * 1024 * 1024,
        name="force",
    )
    force_came = to[4](force_far)
    tail = 8
    group = 4 * rows
    keep, give = call(
        gradient_kernel,
        [((2 * group + tail, hidden),)] * 2,
        (adj, pot, h1, h2, g2, g1, x),
        scratch=[pltpu.VMEM((width, hidden), F32), pltpu.VMEM((hidden, hidden), F32)],
        flops=6 * work * hidden * (width + hidden),
        size=4 * 1024 * 1024,
        name="gradient",
    )

    def halve(keep, came, end, name):
        left = (keep.shape[0] - end) // 2 + end
        return call(halving_kernel, [((left, hidden),)] * 2, (keep, came), size=4 * 4 * left * hidden, name=name)

    far_stay, far_leave, near_stay, near_leave = call(
        core_kernel,
        [((group // 2 + tail, hidden),)] * 2 + [((group // 2, hidden),)] * 2,
        (keep, to_core(give)),
        name="core_sum",
    )
    far_came = to[1](far_leave)
    far_stay, far_leave = halve(far_stay, far_came, tail, "far_x")
    near_came = to[1](after(near_leave, far_came))
    far_came = to[2](far_leave)
    near_stay, near_leave = halve(near_stay, near_came, 0, "near_x")
    token = force_came[0, 0:8, 0:128]
    token = to_core(token)
    (beyond_sum,) = call(sum_kernel, [((rows + tail, hidden),)], (far_stay, far_came, token), name="far_z")
    came = to[4](beyond_sum)
    last_came = to[2](near_leave)
    shape = lambda x: jax.ShapeDtypeStruct(x.shape, F32)
    vec_mom = vector_momentum.transpose(1, 0, 2)
    mine_first, mine_second, force_partials = pl.pallas_call(
        near_kernel,
        out_shape=[
            jax.ShapeDtypeStruct((1, first_layer.shape[1]), F32), jax.ShapeDtypeStruct((1, second_layer.shape[1]), F32),
            shape(descriptors),
        ],
        in_specs=[vmem] * 4,
        out_specs=[vmem] * 2 + [any_space],
        scratch_shapes=[pltpu.VMEM((rows, hidden), F32), pltpu.SemaphoreType.DMA((2,))],
        compiler_params=pltpu.CompilerParams(vmem_limit_bytes=8 * 1024 * 1024),
        cost_estimate=pl.CostEstimate(flops=1, bytes_accessed=1, transcendentals=0),
        name="near_z",
    )(near_stay, last_came, force_near, force_came)
    (
        new_first, new_second, new_vec, new_first_mom, new_second_mom, new_vec_mom, potential,
    ) = pl.pallas_call(
        final_kernel,
        out_shape=[
            shape(first_layer), shape(second_layer), shape(vec), shape(first_layer), shape(second_layer), shape(vec),
            jax.ShapeDtypeStruct((1, 128), F32),
        ],
        in_specs=[vmem] * 10,
        out_specs=[vmem] * 7,
        scratch_shapes=[pltpu.VMEM(first_layer.shape, F32), pltpu.VMEM(second_layer.shape, F32)],
        compiler_params=pltpu.CompilerParams(vmem_limit_bytes=8 * 1024 * 1024),
        cost_estimate=pl.CostEstimate(flops=1, bytes_accessed=1, transcendentals=0),
        name="final",
    )(
        mine_first, mine_second, beyond_sum, came, first_layer, second_layer, vec, first_momentum, second_momentum, vec_mom,
    )
    return (
        new_first, new_second, new_vec.transpose(1, 0, 2), new_first_mom, new_second_mom,
        new_vec_mom.transpose(1, 0, 2), potential[0, 0:1], force_partials,
    )


def element_energies(first, second, vectors, desc):
    lower = jnp.einsum("erf,efj->erj", desc, first, precision=HIGH) + vectors[:, 0][:, None, :]
    hidden = jnp.tanh(lower)
    upper = jnp.einsum("erj,ejk->erk", hidden, second, precision=HIGH) + vectors[:, 1][:, None, :]
    top = jnp.tanh(upper)
    return jnp.einsum("erk,ek->er", top, vectors[:, 2], precision=HIGH)


def structure_terms(energies, live, ids, refs):
    member = (
        ids[..., None] == jnp.arange(refs.shape[0], dtype=jnp.int32)[None, None, None, :]
    ).astype(jnp.float32)
    total = jnp.einsum("ebas,eba->s", member, energies, precision=HIGH)
    count = jnp.maximum(jnp.einsum("ebas,eba->s", member, live, precision=HIGH), 1.0)
    error = total / count - refs
    potential_part = jnp.sum(error * error) / (2.0 * NOISE_VAR)
    scale = error / count / NOISE_VAR
    adjoint = jnp.einsum("ebas,s->eba", member, scale, precision=HIGH) * live
    return (potential_part, adjoint)


def on_device(
    descriptors,
    counts,
    struct_ids,
    ref_energy,
    first_layer,
    second_layer,
    vectors,
    first_momentum,
    second_momentum,
    vector_momentum,
):
    nelem, slots, atoms, width = descriptors.shape
    hidden_width = vectors.shape[2]
    flat_first, flat_second = (
        lax.all_gather(first_layer, ("dp", "rep"), axis=1, tiled=True),
        lax.all_gather(second_layer, ("dp", "rep"), axis=1, tiled=True),
    )
    params = (
        flat_first.reshape(nelem, width, hidden_width),
        flat_second.reshape(nelem, hidden_width, hidden_width),
        vectors,
    )
    positions = jnp.arange(atoms, dtype=jnp.int32)
    live = (positions[None, None, :] < counts[:, :, None]).astype(jnp.float32)

    def forward(block):
        number = block.shape[1]

        def energy_fn(weights, pieces):
            flat = pieces.reshape(nelem, number * atoms, width)
            return element_energies(weights[0], weights[1], weights[2], flat).reshape(
                nelem, number, atoms
            )

        return jax.vjp(energy_fn, params, block)

    raw, pull = forward(descriptors)
    potential_part, adjoint = structure_terms(raw * live, live, struct_ids, ref_energy)
    grads, force_partials = pull(adjoint)
    grad_first = grads[0].reshape(nelem, width * hidden_width)
    grad_second = grads[1].reshape(nelem, hidden_width * hidden_width)
    sum_first, sum_second, grad_vectors, potential_sum = lax.psum(
        (grad_first, grad_second, grads[2], potential_part), ("dp", "rep")
    )
    position = lax.axis_index(("dp", "rep"))
    share_first = lax.dynamic_slice_in_dim(
        sum_first, position * first_layer.shape[1], first_layer.shape[1], 1
    )
    share_second = lax.dynamic_slice_in_dim(
        sum_second, position * second_layer.shape[1], second_layer.shape[1], 1
    )
    new_first_mom = first_momentum - STEP_SIZE * share_first
    new_second_mom = second_momentum - STEP_SIZE * share_second
    new_vector_mom = vector_momentum - STEP_SIZE * grad_vectors
    new_first = first_layer + STEP_SIZE * new_first_mom
    new_second = second_layer + STEP_SIZE * new_second_mom
    new_vectors = vectors + STEP_SIZE * new_vector_mom
    potential = (potential_sum / (ref_energy.shape[0] * lax.axis_size(("dp", "rep")))).reshape(1)
    return (
        new_first,
        new_second,
        new_vectors,
        new_first_mom,
        new_second_mom,
        new_vector_mom,
        potential,
        force_partials,
    )


def solution(mesh):
    placed = (
        P(None, ("dp", "rep"), None, None),
        P(None, ("dp", "rep")),
        P(None, ("dp", "rep"), None),
        P(("dp", "rep")),
        P("chain", ("dp", "rep")),
        P("chain", ("dp", "rep")),
        P("chain", None, None),
        P("chain", ("dp", "rep")),
        P("chain", ("dp", "rep")),
        P("chain", None, None),
    )
    split_by_half = (mesh.shape["chain"], mesh.shape["dp"], mesh.shape["rep"]) == (2, 8, 2)
    return jax.shard_map(
        halves if split_by_half else on_device,
        mesh=mesh,
        in_specs=placed,
        out_specs=(
            P("chain", ("dp", "rep")),
            P("chain", ("dp", "rep")),
            P("chain", None, None),
            P("chain", ("dp", "rep")),
            P("chain", ("dp", "rep")),
            P("chain", None, None),
            P("chain"),
            P("chain", ("dp", "rep"), None, None),
        ),
        check_vma=False,
    )
```

```python
import jax
import jax.numpy as jnp
from jax import lax
from jax.experimental import pallas as pl
from jax.experimental.pallas import tpu as pltpu
from jax.sharding import PartitionSpec as P

NOISE_VAR = 0.1
STEP_SIZE = 0.01
HIGH = lax.Precision.HIGHEST
F32 = jnp.float32
BF16 = jnp.bfloat16
VMEM = pltpu.VMEM
LIMIT = 32 * 1024 * 1024

NT = (((1,), (1,)), ((), ()))
TN = (((0,), (0,)), ((), ()))
NN = (((1,), (0,)), ((), ()))


def split(x):
    high = x.astype(BF16)
    return high, (x - high.astype(F32)).astype(BF16)


def product(left, right, dims):
    one = lambda a, b: lax.dot_general(a, b, dims, preferred_element_type=F32)
    return one(left[0], right[0]) + (one(left[0], right[1]) + one(left[1], right[0]))


def call(kernel, outs, args, scratch=(), flops=0, size=0, name=None):
    return pl.pallas_call(
        kernel,
        out_shape=[jax.ShapeDtypeStruct(shape, kind) for shape, kind in ((*out, F32)[:2] for out in outs)],
        in_specs=[pl.BlockSpec(memory_space=VMEM)] * len(args),
        out_specs=[pl.BlockSpec(memory_space=VMEM)] * len(outs),
        scratch_shapes=list(scratch),
        compiler_params=pltpu.CompilerParams(vmem_limit_bytes=LIMIT),
        cost_estimate=pl.CostEstimate(flops=1, bytes_accessed=1, transcendentals=0),
        name=name,
    )(*args)


def place():
    spot = lax.axis_index("dp")
    return spot, lax.axis_index("rep"), spot // 4, lax.axis_index("chain")


def forward_kernel(
    desc_ref, meta_ref, first_far, second_far, far_meta, vec_ref,
    own0, own1, rec0, rec1,
    h1_ref, h2_ref, x_ref, member_ref, sums_ref, w1h, w1l, w2h, w2l,
):
    spot, core, half, chain = place()
    width = w1h.shape[1]
    rows1 = w1h.shape[0] // 16
    rows2 = w2h.shape[0] // 16
    rows = rows1 + rows2
    for far in range(2):
        for other in range(2):
            block = ((own0, own1), (rec0, rec1))[far][other]
            for delta in range(4):
                owner = ((spot ^ (delta + 4 * far)) * 2 + (core ^ other))
                piece = block[delta * rows : delta * rows + rows1, :]
                high, low = split(piece)
                at = pl.ds(pl.multiple_of(owner * rows1, rows1), rows1)
                w1h[at, :] = high
                w1l[at, :] = low
                piece = block[delta * rows + rows1 : (delta + 1) * rows, :]
                high, low = split(piece)
                at = pl.ds(pl.multiple_of(owner * rows2, rows2), rows2)
                w2h[at, :] = high
                w2l[at, :] = low
    atoms = desc_ref.shape[2]
    near = meta_ref[...]
    away = far_meta[...]
    n_near = [near[1:2, 0:1], near[1:2, 1:2]]
    n_far = [away[1:2, 0:1], away[1:2, 1:2]]
    choose = lambda number, yes, no: jnp.where(jnp.broadcast_to(number, yes.shape) > 0.5, yes, no)
    own_desc = [desc_ref[half, 0], desc_ref[half, 1]]
    direct = first_far[...]
    shared = second_far[...]
    even = chain == 0
    far_desc = [jnp.where(even, direct, shared), jnp.where(even, shared, direct)]
    first = lambda own, far: choose(n_near[0], own[0], far[0])
    second = lambda own, far: choose(n_near[1], own[1], choose(n_near[0], far[0], far[1]))
    x0, x1 = first(own_desc, far_desc), second(own_desc, far_desc)
    n0, n1 = first(n_near, n_far), second(n_near, n_far)
    near_ids = near[0:1, :]
    far_ids = away[0:1, :] + 32.0
    pair = lambda row: [row[:, :atoms], row[:, atoms:]]
    id0, id1 = first(pair(near_ids), pair(far_ids)), second(pair(near_ids), pair(far_ids))
    ids = jnp.broadcast_to(jnp.concatenate([id0, id1], axis=1), (128, 2 * atoms)).T[:, 0:128]
    spots = lax.broadcasted_iota(jnp.int32, (atoms, 128), 0).astype(F32)
    live = jnp.concatenate([(spots < n0).astype(F32), (spots < n1).astype(F32)], axis=0)
    lanes = lax.broadcasted_iota(jnp.int32, (2 * atoms, 128), 1).astype(F32)
    member = jnp.where(ids == lanes, live, 0.0)
    member_ref[...] = member

    x = jnp.concatenate([x0, x1], axis=0)
    x_ref[...] = x
    c1, c2, w3 = [vec_ref[kind, pl.ds(half, 1), :] for kind in range(3)]
    w1 = (w1h[...], w1l[...])
    w2 = (w2h[...], w2l[...])
    h1 = jnp.tanh(product(split(x), w1, NN) + c1)
    h1_ref[...] = h1
    h2 = jnp.tanh(product(split(h1), w2, NN) + c2)
    h2_ref[...] = h2
    energy = jnp.sum(h2 * w3, axis=1, keepdims=True)
    sums_ref[0:1, :] = jnp.sum(member * energy, axis=0, keepdims=True)
    sums_ref[1:2, :] = jnp.sum(member, axis=0, keepdims=True)
    sums_ref[2:8, :] = jnp.zeros((6, 128), F32)


def backward_kernel(h1_ref, h2_ref, vec_ref, w1h, w1l, w2h, w2l, g2_ref, g1_ref, f_ref):
    spot, core, half, chain = place()
    w3 = vec_ref[2, pl.ds(half, 1), :]
    h1, h2 = h1_ref[...], h2_ref[...]
    g2 = w3 * (1.0 - h2 * h2)
    g2_ref[...] = g2
    g1 = product(split(g2), (w2h[...], w2l[...]), NT) * (1.0 - h1 * h1)
    g1_ref[...] = g1
    f_ref[...] = product(split(g1), (w1h[...], w1l[...]), NT)


def force_kernel(mine, theirs, refs, near, member, f_ref, force_near, force_far, adj_ref, pot_ref):
    other = theirs[...]
    lane = lax.broadcasted_iota(jnp.int32, other.shape, 1)
    other = jnp.where(lane < 32, pltpu.roll(other, 96, 1), pltpu.roll(other, 32, 1))
    total = mine[0:1, :] + other[0:1, :]
    count = jnp.maximum(mine[1:2, :] + other[1:2, :], 1.0)
    error = total / count - refs[0:1, :]
    inside = lax.broadcasted_iota(jnp.int32, (1, 128), 1) < 64
    error = jnp.where(inside, error, 0.0)
    square = error * error
    low = jnp.sum(square[:, 0:32], axis=1, keepdims=True)
    high = jnp.sum(square[:, 32:64], axis=1, keepdims=True)
    pot_ref[...] = jnp.broadcast_to((low + high) / (2.0 * NOISE_VAR), (8, 128))
    scale = error / count / NOISE_VAR
    adj = jnp.sum(member[...] * scale, axis=1, keepdims=True)
    adj_ref[...] = jnp.broadcast_to(adj, adj_ref.shape)
    force = adj * f_ref[...]
    atoms = force.shape[0] // 2
    f0, f1 = force[:atoms], force[atoms:]
    has0 = jnp.broadcast_to(near[1:2, 0:1], f0.shape) > 0.5
    has1 = jnp.broadcast_to(near[1:2, 1:2], f0.shape) > 0.5
    force_near[0] = jnp.where(has0, f0, 0.0)
    force_near[1] = jnp.where(has1, f1, 0.0)
    force_far[0] = jnp.where(has0, jnp.where(has1, 0.0, f1), f0)
    force_far[1] = jnp.where(has0, 0.0, f1)


def gradient_kernel(
    adj_ref, pot_ref, h1_ref, h2_ref, g2_ref, g1_ref, x_ref, keep_all, give_all, dw1, dw2,
):
    spot, core, half, chain = place()
    adj = adj_ref[...][:, 0:1]
    g2 = adj * g2_ref[...]
    g1 = adj * g1_ref[...]
    dw2[...] = product(split(h1_ref[...]), split(g2), TN)
    dw1[...] = product(split(x_ref[...]), split(g1), TN)
    rows1 = dw1.shape[0] // 16
    rows2 = dw2.shape[0] // 16
    rows = rows1 + rows2
    middle = 4 * rows + 8
    keep_far, give_far = [ref.at[pl.ds(0, middle)] for ref in (keep_all, give_all)]
    keep_near, give_near = [ref.at[pl.ds(middle, 4 * rows)] for ref in (keep_all, give_all)]
    for far, keep, give in ((4, keep_far, give_far), (0, keep_near, give_near)):
        for index, delta in enumerate((0, 2, 1, 3)):
            for out, holder in ((keep, core), (give, 1 - core)):
                owner = (spot ^ (delta + far)) * 2 + holder
                base = index * rows
                at = pl.ds(pl.multiple_of(owner * rows1, rows1), rows1)
                out[base : base + rows1, :] = dw1[at, :]
                at = pl.ds(pl.multiple_of(owner * rows2, rows2), rows2)
                out[base + rows1 : base + rows, :] = dw2[at, :]
    base = 4 * rows
    width = g2.shape[1]
    vec = [
        jnp.sum(g1, axis=0, keepdims=True),
        jnp.sum(g2, axis=0, keepdims=True),
        jnp.sum(adj * h2_ref[...], axis=0, keepdims=True),
        jnp.broadcast_to(pot_ref[0:1, 0:1], (1, width)),
    ]
    tail = jnp.concatenate(vec + [jnp.zeros((4, width), F32)], axis=0)
    keep_far[base : base + 8, :] = tail
    give_far[base : base + 8, :] = tail


def halving_kernel(keep, came, stay, leave):
    tail = stay.shape[0] % 48
    rows = stay.shape[0] - tail
    stay[0:rows, :] = keep[0:rows, :] + came[0:rows, :]
    leave[0:rows, :] = keep[rows : 2 * rows, :] + came[rows : 2 * rows, :]
    if tail:
        end = keep[2 * rows :, :] + came[2 * rows :, :]
        stay[rows:, :] = end
        leave[rows:, :] = end


def core_kernel(keep, came, far_stay, far_leave, near_stay, near_leave):
    half_rows = near_stay.shape[0]
    tail = far_stay.shape[0] - half_rows
    far_rows = 2 * half_rows + tail
    total = lambda start, rows: keep[start : start + rows, :] + came[start : start + rows, :]
    far_stay[0:half_rows, :] = total(0, half_rows)
    far_leave[0:half_rows, :] = total(half_rows, half_rows)
    end = total(2 * half_rows, tail)
    far_stay[half_rows:, :] = end
    far_leave[half_rows:, :] = end
    near_stay[...] = total(far_rows, half_rows)
    near_leave[...] = total(far_rows + half_rows, half_rows)


def sum_kernel(a, b, *rest):
    out = rest[-1]
    out[...] = a[...] + b[...]


def message_kernel(
    desc_hbm, counts_hbm, ids_hbm, refs_hbm, vec_hbm, message, near, vec, counts, ids, refs, sems,
):
    spot, core, half, chain = place()
    atoms = message.shape[0] - 8
    loads = [
        pltpu.make_async_copy(source, target, sems.at[index])
        for index, (source, target) in enumerate(
            (
                (counts_hbm, counts),
                (ids_hbm, ids),
                (refs_hbm, refs),
                (vec_hbm, vec),
                (desc_hbm.at[1 - half, chain], message.at[pl.ds(0, atoms)]),
            )
        )
    ]
    for load in loads:
        load.start()
    for load in loads:
        load.wait()
    for out, base, element in ((near, 0, half), (message, atoms, 1 - half)):
        out[base : base + 8, :] = jnp.zeros((8, 2 * atoms), F32)
        row = ids[element].astype(F32)
        out[base : base + 1, 0:atoms] = row[0:1]
        out[base : base + 1, atoms:] = row[1:2]
        number = counts[pl.ds(element, 1), :].astype(F32)
        out[base + 1 : base + 2, 0:2] = number
        out[base + 2 : base + 3, 0 : refs.shape[1]] = refs[...]


def near_kernel(a, b, force_near, force_came, mine_first, mine_second, forces, total, sems):
    spot, core, half, chain = place()
    near_copy = pltpu.make_async_copy(force_near, forces.at[half], sems.at[0])
    far_copy = pltpu.make_async_copy(force_came, forces.at[1 - half], sems.at[1])
    near_copy.start()
    far_copy.start()
    total[...] = a[...] + b[...]
    hidden = total.shape[1]
    rows1 = mine_first.shape[1] // hidden
    rows2 = mine_second.shape[1] // hidden
    for row in range(rows1):
        mine_first[:, row * hidden : (row + 1) * hidden] = total[row : row + 1, :]
    for row in range(rows2):
        mine_second[:, row * hidden : (row + 1) * hidden] = total[rows1 + row : rows1 + row + 1, :]
    near_copy.wait()
    far_copy.wait()


def final_kernel(
    mine_first, mine_second, beyond, came, first, second, vec, first_mom, second_mom, vec_mom,
    new_first, new_second, new_vec, new_first_mom, new_second_mom, new_vec_mom, potential,
    flat_first, flat_second,
):
    spot, core, half, chain = place()
    hidden = came.shape[1]
    rows1 = flat_first.shape[1] // hidden
    rows2 = flat_second.shape[1] // hidden
    rows = rows1 + rows2
    flat_first[pl.ds(half, 1), :] = mine_first[...]
    flat_second[pl.ds(half, 1), :] = mine_second[...]
    for row in range(rows1):
        flat_first[pl.ds(1 - half, 1), row * hidden : (row + 1) * hidden] = came[row : row + 1, :]
    for row in range(rows2):
        flat_second[pl.ds(1 - half, 1), row * hidden : (row + 1) * hidden] = came[rows1 + row : rows1 + row + 1, :]
    for grad, value, momentum, new_value, new_momentum in (
        (flat_first, first, first_mom, new_first, new_first_mom),
        (flat_second, second, second_mom, new_second, new_second_mom),
    ):
        moved = momentum[...] - STEP_SIZE * grad[...]
        new_momentum[...] = moved
        new_value[...] = value[...] + STEP_SIZE * moved
    low = jnp.full((1, hidden), half, jnp.int32) == 0
    for kind in range(3):
        own = beyond[rows + kind : rows + kind + 1, :]
        other = came[rows + kind : rows + kind + 1, :]
        for element in range(2):
            grad = jnp.where(low, own, other) if element == 0 else jnp.where(low, other, own)
            moved = vec_mom[kind, element : element + 1, :] - STEP_SIZE * grad
            new_vec_mom[kind, element : element + 1, :] = moved
            new_vec[kind, element : element + 1, :] = vec[kind, element : element + 1, :] + STEP_SIZE * moved
    potential[...] = beyond[rows + 3 : rows + 4, 0:128] * (1.0 / 512.0)


def after(value, *others):
    return lax.optimization_barrier((value,) + others)[0]


def flip(axis, delta, size):
    return lambda x: lax.ppermute(x, axis, [(i, i ^ delta) for i in range(size)])


def halves(
    descriptors, counts, struct_ids, ref_energy, first_layer, second_layer, vectors,
    first_momentum, second_momentum, vector_momentum,
):
    nelem, slots, atoms, width = descriptors.shape
    hidden = vectors.shape[2]
    structs = ref_energy.shape[0]
    spot, core, half, chain = place()
    to = [None] + [flip("dp", delta, 8) for delta in range(1, 8)]
    to_core = flip("rep", 1, 2)
    to_chain = flip("chain", 1, 2)
    rows1 = first_layer.shape[1] // hidden
    rows2 = second_layer.shape[1] // hidden
    rows = rows1 + rows2
    shards = jnp.concatenate(
        [first_layer.reshape(nelem, rows1, hidden), second_layer.reshape(nelem, rows2, hidden)], axis=1
    )
    pick = lambda x, at: lax.dynamic_index_in_dim(x, at, 0, keepdims=False)
    own = pick(shards, half)
    got = to[4](pick(shards, 1 - half))

    any_space = pl.BlockSpec(memory_space=pl.ANY)
    vmem = pl.BlockSpec(memory_space=VMEM)
    message, meta, vec = pl.pallas_call(
        message_kernel,
        out_shape=[jax.ShapeDtypeStruct((atoms + 8, width), F32), jax.ShapeDtypeStruct((8, width), F32),
            jax.ShapeDtypeStruct((3, nelem, hidden), F32),
        ],
        in_specs=[pl.BlockSpec(memory_space=pltpu.HBM)] * 5,
        out_specs=[vmem] * 3,
        scratch_shapes=[
            pltpu.VMEM(counts.shape, jnp.int32), pltpu.VMEM(struct_ids.shape, jnp.int32), pltpu.VMEM((1, structs), F32),
            pltpu.SemaphoreType.DMA((5,)),
        ],
        compiler_params=pltpu.CompilerParams(vmem_limit_bytes=4 * 1024 * 1024),
        name="message",
    )(descriptors, counts, struct_ids, ref_energy.reshape(1, structs), vectors.transpose(1, 0, 2))
    message = to[4](message)
    own_z = to[2](own)
    own_x = to[1](jnp.concatenate([own, own_z]))
    own_came = [own_x[:rows], own_z, own_x[rows:]]
    got = after(got, own)
    direct = message[:atoms]
    far_meta = message[atoms:]
    shared = to_chain(direct)
    own_set = jnp.concatenate(lax.optimization_barrier((own, *own_came, got))[:4], axis=0)
    own_across = to_core(after(own_set, message))
    got_z = to[2](got)
    got_x = to[1](jnp.concatenate([got, got_z]))
    got_set = jnp.concatenate([got, got_x[:rows], got_z, got_x[rows:]], axis=0)
    near_across = to_core(after(jnp.concatenate([got, got_z]), message))
    last_across = to_core(after(got_x, shared))
    got_across = jnp.concatenate([near_across[:rows], last_across[:rows], near_across[rows:], last_across[rows:]], axis=0)

    work = slots * atoms
    h1, h2, x, member, sums, *weights = call(
        forward_kernel,
        [((work, hidden),)] * 2 + [((work, width),), ((work, 128),), ((8, 128),)]
        + [((width, hidden), BF16)] * 2 + [((hidden, hidden), BF16)] * 2,
        (descriptors, meta, direct, shared, far_meta, vec, own_set, own_across, got_set, got_across),
        flops=6 * work * hidden * (width + hidden),
        size=6 * 1024 * 1024,
        name="forward",
    )
    sums_came = to[4](sums)
    g2, g1, f = call(
        backward_kernel,
        [((work, hidden),)] * 2 + [((work, width),)],
        (h1, h2, vec, *weights),
        flops=6 * work * hidden * (width + hidden),
        size=6 * 1024 * 1024,
        name="backward",
    )
    refs = jnp.concatenate([meta[2:3, 0:structs], far_meta[2:3, 0:structs], jnp.zeros((1, 128 - 2 * structs), F32)], axis=1)
    force_near, force_far, adj, pot = call(
        force_kernel,
        [((slots, atoms, width),)] * 2 + [((work, 128),), ((8, 128),)],
        (sums, sums_came, refs, meta, member, f),
        size=2 * 1024 * 1024,
        name="force",
    )
    force_came = to[4](force_far)
    tail = 8
    group = 4 * rows
    keep, give = call(
        gradient_kernel,
        [((2 * group + tail, hidden),)] * 2,
        (adj, pot, h1, h2, g2, g1, x),
        scratch=[pltpu.VMEM((width, hidden), F32), pltpu.VMEM((hidden, hidden), F32)],
        flops=6 * work * hidden * (width + hidden),
        size=4 * 1024 * 1024,
        name="gradient",
    )

    def halve(keep, came, end, name):
        left = (keep.shape[0] - end) // 2 + end
        return call(halving_kernel, [((left, hidden),)] * 2, (keep, came), size=4 * 4 * left * hidden, name=name)

    far_stay, far_leave, near_stay, near_leave = call(
        core_kernel,
        [((group // 2 + tail, hidden),)] * 2 + [((group // 2, hidden),)] * 2,
        (keep, to_core(give)),
        name="core_sum",
    )
    far_came = to[1](far_leave)
    far_stay, far_leave = halve(far_stay, far_came, tail, "far_x")
    near_came = to[1](near_leave)
    far_came = to[2](far_leave)
    near_stay, near_leave = halve(near_stay, near_came, 0, "near_x")
    token = force_came[0, 0:8, 0:128]
    token = to_core(token)
    (beyond_sum,) = call(sum_kernel, [((rows + tail, hidden),)], (far_stay, far_came, token), name="far_z")
    came = to[4](beyond_sum)
    last_came = to[2](near_leave)
    shape = lambda x: jax.ShapeDtypeStruct(x.shape, F32)
    vec_mom = vector_momentum.transpose(1, 0, 2)
    mine_first, mine_second, force_partials = pl.pallas_call(
        near_kernel,
        out_shape=[
            jax.ShapeDtypeStruct((1, first_layer.shape[1]), F32), jax.ShapeDtypeStruct((1, second_layer.shape[1]), F32),
            shape(descriptors),
        ],
        in_specs=[vmem] * 4,
        out_specs=[vmem] * 2 + [any_space],
        scratch_shapes=[pltpu.VMEM((rows, hidden), F32), pltpu.SemaphoreType.DMA((2,))],
        compiler_params=pltpu.CompilerParams(vmem_limit_bytes=8 * 1024 * 1024),
        cost_estimate=pl.CostEstimate(flops=1, bytes_accessed=1, transcendentals=0),
        name="near_z",
    )(near_stay, last_came, force_near, force_came)
    (
        new_first, new_second, new_vec, new_first_mom, new_second_mom, new_vec_mom, potential,
    ) = pl.pallas_call(
        final_kernel,
        out_shape=[
            shape(first_layer), shape(second_layer), shape(vec), shape(first_layer), shape(second_layer), shape(vec),
            jax.ShapeDtypeStruct((1, 128), F32),
        ],
        in_specs=[vmem] * 10,
        out_specs=[vmem] * 7,
        scratch_shapes=[pltpu.VMEM(first_layer.shape, F32), pltpu.VMEM(second_layer.shape, F32)],
        compiler_params=pltpu.CompilerParams(vmem_limit_bytes=8 * 1024 * 1024),
        cost_estimate=pl.CostEstimate(flops=1, bytes_accessed=1, transcendentals=0),
        name="final",
    )(
        mine_first, mine_second, beyond_sum, came, first_layer, second_layer, vec, first_momentum, second_momentum, vec_mom,
    )
    return (
        new_first, new_second, new_vec.transpose(1, 0, 2), new_first_mom, new_second_mom,
        new_vec_mom.transpose(1, 0, 2), potential[0, 0:1], force_partials,
    )


def element_energies(first, second, vectors, desc):
    lower = jnp.einsum("erf,efj->erj", desc, first, precision=HIGH) + vectors[:, 0][:, None, :]
    hidden = jnp.tanh(lower)
    upper = jnp.einsum("erj,ejk->erk", hidden, second, precision=HIGH) + vectors[:, 1][:, None, :]
    top = jnp.tanh(upper)
    return jnp.einsum("erk,ek->er", top, vectors[:, 2], precision=HIGH)


def structure_terms(energies, live, ids, refs):
    member = (
        ids[..., None] == jnp.arange(refs.shape[0], dtype=jnp.int32)[None, None, None, :]
    ).astype(jnp.float32)
    total = jnp.einsum("ebas,eba->s", member, energies, precision=HIGH)
    count = jnp.maximum(jnp.einsum("ebas,eba->s", member, live, precision=HIGH), 1.0)
    error = total / count - refs
    potential_part = jnp.sum(error * error) / (2.0 * NOISE_VAR)
    scale = error / count / NOISE_VAR
    adjoint = jnp.einsum("ebas,s->eba", member, scale, precision=HIGH) * live
    return (potential_part, adjoint)


def on_device(
    descriptors,
    counts,
    struct_ids,
    ref_energy,
    first_layer,
    second_layer,
    vectors,
    first_momentum,
    second_momentum,
    vector_momentum,
):
    nelem, slots, atoms, width = descriptors.shape
    hidden_width = vectors.shape[2]
    flat_first, flat_second = (
        lax.all_gather(first_layer, ("dp", "rep"), axis=1, tiled=True),
        lax.all_gather(second_layer, ("dp", "rep"), axis=1, tiled=True),
    )
    params = (
        flat_first.reshape(nelem, width, hidden_width),
        flat_second.reshape(nelem, hidden_width, hidden_width),
        vectors,
    )
    positions = jnp.arange(atoms, dtype=jnp.int32)
    live = (positions[None, None, :] < counts[:, :, None]).astype(jnp.float32)

    def forward(block):
        number = block.shape[1]

        def energy_fn(weights, pieces):
            flat = pieces.reshape(nelem, number * atoms, width)
            return element_energies(weights[0], weights[1], weights[2], flat).reshape(
                nelem, number, atoms
            )

        return jax.vjp(energy_fn, params, block)

    raw, pull = forward(descriptors)
    potential_part, adjoint = structure_terms(raw * live, live, struct_ids, ref_energy)
    grads, force_partials = pull(adjoint)
    grad_first = grads[0].reshape(nelem, width * hidden_width)
    grad_second = grads[1].reshape(nelem, hidden_width * hidden_width)
    sum_first, sum_second, grad_vectors, potential_sum = lax.psum(
        (grad_first, grad_second, grads[2], potential_part), ("dp", "rep")
    )
    position = lax.axis_index(("dp", "rep"))
    share_first = lax.dynamic_slice_in_dim(
        sum_first, position * first_layer.shape[1], first_layer.shape[1], 1
    )
    share_second = lax.dynamic_slice_in_dim(
        sum_second, position * second_layer.shape[1], second_layer.shape[1], 1
    )
    new_first_mom = first_momentum - STEP_SIZE * share_first
    new_second_mom = second_momentum - STEP_SIZE * share_second
    new_vector_mom = vector_momentum - STEP_SIZE * grad_vectors
    new_first = first_layer + STEP_SIZE * new_first_mom
    new_second = second_layer + STEP_SIZE * new_second_mom
    new_vectors = vectors + STEP_SIZE * new_vector_mom
    potential = (potential_sum / (ref_energy.shape[0] * lax.axis_size(("dp", "rep")))).reshape(1)
    return (
        new_first,
        new_second,
        new_vectors,
        new_first_mom,
        new_second_mom,
        new_vector_mom,
        potential,
        force_partials,
    )


def solution(mesh):
    placed = (
        P(None, ("dp", "rep"), None, None),
        P(None, ("dp", "rep")),
        P(None, ("dp", "rep"), None),
        P(("dp", "rep")),
        P("chain", ("dp", "rep")),
        P("chain", ("dp", "rep")),
        P("chain", None, None),
        P("chain", ("dp", "rep")),
        P("chain", ("dp", "rep")),
        P("chain", None, None),
    )
    split_by_half = (mesh.shape["chain"], mesh.shape["dp"], mesh.shape["rep"]) == (2, 8, 2)
    return jax.shard_map(
        halves if split_by_half else on_device,
        mesh=mesh,
        in_specs=placed,
        out_specs=(
            P("chain", ("dp", "rep")),
            P("chain", ("dp", "rep")),
            P("chain", None, None),
            P("chain", ("dp", "rep")),
            P("chain", ("dp", "rep")),
            P("chain", None, None),
            P("chain"),
            P("chain", ("dp", "rep"), None, None),
        ),
        check_vma=False,
    )
```

```python
import jax
import jax.numpy as jnp
from jax import lax
from jax.experimental import pallas as pl
from jax.experimental.pallas import tpu as pltpu
from jax.sharding import PartitionSpec as P

NOISE_VAR = 0.1
STEP_SIZE = 0.01
HIGH = lax.Precision.HIGHEST
F32 = jnp.float32
BF16 = jnp.bfloat16
VMEM = pltpu.VMEM
LIMIT = 32 * 1024 * 1024

NT = (((1,), (1,)), ((), ()))
TN = (((0,), (0,)), ((), ()))
NN = (((1,), (0,)), ((), ()))


def split(x):
    high = x.astype(BF16)
    return high, (x - high.astype(F32)).astype(BF16)


def product(left, right, dims):
    one = lambda a, b: lax.dot_general(a, b, dims, preferred_element_type=F32)
    return one(left[0], right[0]) + (one(left[0], right[1]) + one(left[1], right[0]))


def call(kernel, outs, args, scratch=(), flops=0, size=0, name=None):
    return pl.pallas_call(
        kernel,
        out_shape=[jax.ShapeDtypeStruct(shape, kind) for shape, kind in ((*out, F32)[:2] for out in outs)],
        in_specs=[pl.BlockSpec(memory_space=VMEM)] * len(args),
        out_specs=[pl.BlockSpec(memory_space=VMEM)] * len(outs),
        scratch_shapes=list(scratch),
        compiler_params=pltpu.CompilerParams(vmem_limit_bytes=LIMIT),
        cost_estimate=pl.CostEstimate(flops=1, bytes_accessed=1, transcendentals=0),
        name=name,
    )(*args)


def place():
    spot = lax.axis_index("dp")
    return spot, lax.axis_index("rep"), spot // 4, lax.axis_index("chain")


def forward_kernel(
    desc_ref, meta_ref, first_far, second_far, far_meta, vec_ref,
    own0, own1, rec0, rec1,
    h1_ref, h2_ref, x_ref, member_ref, sums_ref, w1h, w1l, w2h, w2l,
):
    spot, core, half, chain = place()
    width = w1h.shape[1]
    rows1 = w1h.shape[0] // 16
    rows2 = w2h.shape[0] // 16
    rows = rows1 + rows2
    for far in range(2):
        for other in range(2):
            block = ((own0, own1), (rec0, rec1))[far][other]
            for delta in range(4):
                owner = ((spot ^ (delta + 4 * far)) * 2 + (core ^ other))
                piece = block[delta * rows : delta * rows + rows1, :]
                high, low = split(piece)
                at = pl.ds(pl.multiple_of(owner * rows1, rows1), rows1)
                w1h[at, :] = high
                w1l[at, :] = low
                piece = block[delta * rows + rows1 : (delta + 1) * rows, :]
                high, low = split(piece)
                at = pl.ds(pl.multiple_of(owner * rows2, rows2), rows2)
                w2h[at, :] = high
                w2l[at, :] = low
    atoms = desc_ref.shape[2]
    near = meta_ref[...]
    away = far_meta[...]
    n_near = [near[1:2, 0:1], near[1:2, 1:2]]
    n_far = [away[1:2, 0:1], away[1:2, 1:2]]
    choose = lambda number, yes, no: jnp.where(jnp.broadcast_to(number, yes.shape) > 0.5, yes, no)
    own_desc = [desc_ref[half, 0], desc_ref[half, 1]]
    direct = first_far[...]
    shared = second_far[...]
    even = chain == 0
    far_desc = [jnp.where(even, direct, shared), jnp.where(even, shared, direct)]
    first = lambda own, far: choose(n_near[0], own[0], far[0])
    second = lambda own, far: choose(n_near[1], own[1], choose(n_near[0], far[0], far[1]))
    x0, x1 = first(own_desc, far_desc), second(own_desc, far_desc)
    n0, n1 = first(n_near, n_far), second(n_near, n_far)
    near_ids = near[0:1, :]
    far_ids = away[0:1, :] + 32.0
    pair = lambda row: [row[:, :atoms], row[:, atoms:]]
    id0, id1 = first(pair(near_ids), pair(far_ids)), second(pair(near_ids), pair(far_ids))
    ids = jnp.broadcast_to(jnp.concatenate([id0, id1], axis=1), (128, 2 * atoms)).T[:, 0:128]
    spots = lax.broadcasted_iota(jnp.int32, (atoms, 128), 0).astype(F32)
    live = jnp.concatenate([(spots < n0).astype(F32), (spots < n1).astype(F32)], axis=0)
    lanes = lax.broadcasted_iota(jnp.int32, (2 * atoms, 128), 1).astype(F32)
    member = jnp.where(ids == lanes, live, 0.0)
    member_ref[...] = member

    x = jnp.concatenate([x0, x1], axis=0)
    x_ref[...] = x
    c1, c2, w3 = [vec_ref[kind, pl.ds(half, 1), :] for kind in range(3)]
    w1 = (w1h[...], w1l[...])
    w2 = (w2h[...], w2l[...])
    h1 = jnp.tanh(product(split(x), w1, NN) + c1)
    h1_ref[...] = h1
    h2 = jnp.tanh(product(split(h1), w2, NN) + c2)
    h2_ref[...] = h2
    energy = jnp.sum(h2 * w3, axis=1, keepdims=True)
    sums_ref[0:1, :] = jnp.sum(member * energy, axis=0, keepdims=True)
    sums_ref[1:2, :] = jnp.sum(member, axis=0, keepdims=True)
    sums_ref[2:8, :] = jnp.zeros((6, 128), F32)


def backward_kernel(h1_ref, h2_ref, vec_ref, w1h, w1l, w2h, w2l, g2_ref, g1_ref, f_ref):
    spot, core, half, chain = place()
    w3 = vec_ref[2, pl.ds(half, 1), :]
    h1, h2 = h1_ref[...], h2_ref[...]
    g2 = w3 * (1.0 - h2 * h2)
    g2_ref[...] = g2
    g1 = product(split(g2), (w2h[...], w2l[...]), NT) * (1.0 - h1 * h1)
    g1_ref[...] = g1
    f_ref[...] = product(split(g1), (w1h[...], w1l[...]), NT)


def force_kernel(mine, theirs, refs, near, member, f_ref, force_near, force_far, adj_ref, pot_ref):
    other = theirs[...]
    lane = lax.broadcasted_iota(jnp.int32, other.shape, 1)
    other = jnp.where(lane < 32, pltpu.roll(other, 96, 1), pltpu.roll(other, 32, 1))
    total = mine[0:1, :] + other[0:1, :]
    count = jnp.maximum(mine[1:2, :] + other[1:2, :], 1.0)
    error = total / count - refs[0:1, :]
    inside = lax.broadcasted_iota(jnp.int32, (1, 128), 1) < 64
    error = jnp.where(inside, error, 0.0)
    square = error * error
    low = jnp.sum(square[:, 0:32], axis=1, keepdims=True)
    high = jnp.sum(square[:, 32:64], axis=1, keepdims=True)
    pot_ref[...] = jnp.broadcast_to((low + high) / (2.0 * NOISE_VAR), (8, 128))
    scale = error / count / NOISE_VAR
    adj = jnp.sum(member[...] * scale, axis=1, keepdims=True)
    adj_ref[...] = jnp.broadcast_to(adj, adj_ref.shape)
    force = adj * f_ref[...]
    atoms = force.shape[0] // 2
    f0, f1 = force[:atoms], force[atoms:]
    has0 = jnp.broadcast_to(near[1:2, 0:1], f0.shape) > 0.5
    has1 = jnp.broadcast_to(near[1:2, 1:2], f0.shape) > 0.5
    force_near[0] = jnp.where(has0, f0, 0.0)
    force_near[1] = jnp.where(has1, f1, 0.0)
    force_far[0] = jnp.where(has0, jnp.where(has1, 0.0, f1), f0)
    force_far[1] = jnp.where(has0, 0.0, f1)


def gradient_kernel(
    adj_ref, pot_ref, h1_ref, h2_ref, g2_ref, g1_ref, x_ref, keep_all, give_all, dw1, dw2,
):
    spot, core, half, chain = place()
    adj = adj_ref[...][:, 0:1]
    g2 = adj * g2_ref[...]
    g1 = adj * g1_ref[...]
    dw2[...] = product(split(h1_ref[...]), split(g2), TN)
    dw1[...] = product(split(x_ref[...]), split(g1), TN)
    rows1 = dw1.shape[0] // 16
    rows2 = dw2.shape[0] // 16
    rows = rows1 + rows2
    middle = 4 * rows + 8
    keep_far, give_far = [ref.at[pl.ds(0, middle)] for ref in (keep_all, give_all)]
    keep_near, give_near = [ref.at[pl.ds(middle, 4 * rows)] for ref in (keep_all, give_all)]
    for far, keep, give in ((4, keep_far, give_far), (0, keep_near, give_near)):
        for index, delta in enumerate((0, 2, 1, 3)):
            for out, holder in ((keep, core), (give, 1 - core)):
                owner = (spot ^ (delta + far)) * 2 + holder
                base = index * rows
                at = pl.ds(pl.multiple_of(owner * rows1, rows1), rows1)
                out[base : base + rows1, :] = dw1[at, :]
                at = pl.ds(pl.multiple_of(owner * rows2, rows2), rows2)
                out[base + rows1 : base + rows, :] = dw2[at, :]
    base = 4 * rows
    width = g2.shape[1]
    vec = [
        jnp.sum(g1, axis=0, keepdims=True),
        jnp.sum(g2, axis=0, keepdims=True),
        jnp.sum(adj * h2_ref[...], axis=0, keepdims=True),
        jnp.broadcast_to(pot_ref[0:1, 0:1], (1, width)),
    ]
    tail = jnp.concatenate(vec + [jnp.zeros((4, width), F32)], axis=0)
    keep_far[base : base + 8, :] = tail
    give_far[base : base + 8, :] = tail


def halving_kernel(keep, came, stay, leave):
    tail = stay.shape[0] % 48
    rows = stay.shape[0] - tail
    stay[0:rows, :] = keep[0:rows, :] + came[0:rows, :]
    leave[0:rows, :] = keep[rows : 2 * rows, :] + came[rows : 2 * rows, :]
    if tail:
        end = keep[2 * rows :, :] + came[2 * rows :, :]
        stay[rows:, :] = end
        leave[rows:, :] = end


def core_kernel(keep, came, far_stay, far_leave, near_stay, near_leave):
    half_rows = near_stay.shape[0]
    tail = far_stay.shape[0] - half_rows
    far_rows = 2 * half_rows + tail
    total = lambda start, rows: keep[start : start + rows, :] + came[start : start + rows, :]
    far_stay[0:half_rows, :] = total(0, half_rows)
    far_leave[0:half_rows, :] = total(half_rows, half_rows)
    end = total(2 * half_rows, tail)
    far_stay[half_rows:, :] = end
    far_leave[half_rows:, :] = end
    near_stay[...] = total(far_rows, half_rows)
    near_leave[...] = total(far_rows + half_rows, half_rows)


def sum_kernel(a, b, *rest):
    out = rest[-1]
    out[...] = a[...] + b[...]


def message_kernel(
    desc_hbm, counts_hbm, ids_hbm, refs_hbm, vec_hbm, message, near, vec, counts, ids, refs, sems,
):
    spot, core, half, chain = place()
    atoms = message.shape[0] - 8
    loads = [
        pltpu.make_async_copy(source, target, sems.at[index])
        for index, (source, target) in enumerate(
            (
                (counts_hbm, counts),
                (ids_hbm, ids),
                (refs_hbm, refs),
                (vec_hbm, vec),
                (desc_hbm.at[1 - half, chain], message.at[pl.ds(0, atoms)]),
            )
        )
    ]
    for load in loads:
        load.start()
    for load in loads:
        load.wait()
    for out, base, element in ((near, 0, half), (message, atoms, 1 - half)):
        out[base : base + 8, :] = jnp.zeros((8, 2 * atoms), F32)
        row = ids[element].astype(F32)
        out[base : base + 1, 0:atoms] = row[0:1]
        out[base : base + 1, atoms:] = row[1:2]
        number = counts[pl.ds(element, 1), :].astype(F32)
        out[base + 1 : base + 2, 0:2] = number
        out[base + 2 : base + 3, 0 : refs.shape[1]] = refs[...]


def near_kernel(a, b, force_near, force_came, mine_first, mine_second, forces, total, sems):
    spot, core, half, chain = place()
    near_copy = pltpu.make_async_copy(force_near, forces.at[half], sems.at[0])
    far_copy = pltpu.make_async_copy(force_came, forces.at[1 - half], sems.at[1])
    near_copy.start()
    far_copy.start()
    total[...] = a[...] + b[...]
    hidden = total.shape[1]
    rows1 = mine_first.shape[1] // hidden
    rows2 = mine_second.shape[1] // hidden
    for row in range(rows1):
        mine_first[:, row * hidden : (row + 1) * hidden] = total[row : row + 1, :]
    for row in range(rows2):
        mine_second[:, row * hidden : (row + 1) * hidden] = total[rows1 + row : rows1 + row + 1, :]
    near_copy.wait()
    far_copy.wait()


def final_kernel(
    mine_first, mine_second, beyond, came, first, second, vec, first_mom, second_mom, vec_mom,
    new_first, new_second, new_vec, new_first_mom, new_second_mom, new_vec_mom, potential,
    flat_first, flat_second,
):
    spot, core, half, chain = place()
    hidden = came.shape[1]
    rows1 = flat_first.shape[1] // hidden
    rows2 = flat_second.shape[1] // hidden
    rows = rows1 + rows2
    flat_first[pl.ds(half, 1), :] = mine_first[...]
    flat_second[pl.ds(half, 1), :] = mine_second[...]
    for row in range(rows1):
        flat_first[pl.ds(1 - half, 1), row * hidden : (row + 1) * hidden] = came[row : row + 1, :]
    for row in range(rows2):
        flat_second[pl.ds(1 - half, 1), row * hidden : (row + 1) * hidden] = came[rows1 + row : rows1 + row + 1, :]
    for grad, value, momentum, new_value, new_momentum in (
        (flat_first, first, first_mom, new_first, new_first_mom),
        (flat_second, second, second_mom, new_second, new_second_mom),
    ):
        moved = momentum[...] - STEP_SIZE * grad[...]
        new_momentum[...] = moved
        new_value[...] = value[...] + STEP_SIZE * moved
    low = jnp.full((1, hidden), half, jnp.int32) == 0
    for kind in range(3):
        own = beyond[rows + kind : rows + kind + 1, :]
        other = came[rows + kind : rows + kind + 1, :]
        for element in range(2):
            grad = jnp.where(low, own, other) if element == 0 else jnp.where(low, other, own)
            moved = vec_mom[kind, element : element + 1, :] - STEP_SIZE * grad
            new_vec_mom[kind, element : element + 1, :] = moved
            new_vec[kind, element : element + 1, :] = vec[kind, element : element + 1, :] + STEP_SIZE * moved
    potential[...] = beyond[rows + 3 : rows + 4, 0:128] * (1.0 / 512.0)


def after(value, *others):
    return lax.optimization_barrier((value,) + others)[0]


def flip(axis, delta, size):
    return lambda x: lax.ppermute(x, axis, [(i, i ^ delta) for i in range(size)])


def halves(
    descriptors, counts, struct_ids, ref_energy, first_layer, second_layer, vectors,
    first_momentum, second_momentum, vector_momentum,
):
    nelem, slots, atoms, width = descriptors.shape
    hidden = vectors.shape[2]
    structs = ref_energy.shape[0]
    spot, core, half, chain = place()
    to = [None] + [flip("dp", delta, 8) for delta in range(1, 8)]
    to_core = flip("rep", 1, 2)
    to_chain = flip("chain", 1, 2)
    rows1 = first_layer.shape[1] // hidden
    rows2 = second_layer.shape[1] // hidden
    rows = rows1 + rows2
    shards = jnp.concatenate(
        [first_layer.reshape(nelem, rows1, hidden), second_layer.reshape(nelem, rows2, hidden)], axis=1
    )
    pick = lambda x, at: lax.dynamic_index_in_dim(x, at, 0, keepdims=False)
    own = pick(shards, half)
    got = to[4](pick(shards, 1 - half))

    any_space = pl.BlockSpec(memory_space=pl.ANY)
    vmem = pl.BlockSpec(memory_space=VMEM)
    message, meta, vec = pl.pallas_call(
        message_kernel,
        out_shape=[jax.ShapeDtypeStruct((atoms + 8, width), F32), jax.ShapeDtypeStruct((8, width), F32),
            jax.ShapeDtypeStruct((3, nelem, hidden), F32),
        ],
        in_specs=[pl.BlockSpec(memory_space=pltpu.HBM)] * 5,
        out_specs=[vmem] * 3,
        scratch_shapes=[
            pltpu.VMEM(counts.shape, jnp.int32), pltpu.VMEM(struct_ids.shape, jnp.int32), pltpu.VMEM((1, structs), F32),
            pltpu.SemaphoreType.DMA((5,)),
        ],
        compiler_params=pltpu.CompilerParams(vmem_limit_bytes=4 * 1024 * 1024),
        name="message",
    )(descriptors, counts, struct_ids, ref_energy.reshape(1, structs), vectors.transpose(1, 0, 2))
    message = to[4](message)
    own_z = to[2](after(own, meta))
    own_x = to[1](jnp.concatenate([own, own_z]))
    own_came = [own_x[:rows], own_z, own_x[rows:]]
    got = after(got, own)
    direct = message[:atoms]
    far_meta = message[atoms:]
    shared = to_chain(direct)
    own_set = jnp.concatenate(lax.optimization_barrier((own, *own_came, got))[:4], axis=0)
    own_across = to_core(after(own_set, message))
    got_z = to[2](got)
    got_x = to[1](jnp.concatenate([got, got_z]))
    got_set = jnp.concatenate([got, got_x[:rows], got_z, got_x[rows:]], axis=0)
    near_across = to_core(after(jnp.concatenate([got, got_z]), message))
    last_across = to_core(after(got_x, shared))
    got_across = jnp.concatenate([near_across[:rows], last_across[:rows], near_across[rows:], last_across[rows:]], axis=0)

    work = slots * atoms
    h1, h2, x, member, sums, *weights = call(
        forward_kernel,
        [((work, hidden),)] * 2 + [((work, width),), ((work, 128),), ((8, 128),)]
        + [((width, hidden), BF16)] * 2 + [((hidden, hidden), BF16)] * 2,
        (descriptors, meta, direct, shared, far_meta, vec, own_set, own_across, got_set, got_across),
        flops=6 * work * hidden * (width + hidden),
        size=6 * 1024 * 1024,
        name="forward",
    )
    sums_came = to[4](sums)
    g2, g1, f = call(
        backward_kernel,
        [((work, hidden),)] * 2 + [((work, width),)],
        (h1, h2, vec, *weights),
        flops=6 * work * hidden * (width + hidden),
        size=6 * 1024 * 1024,
        name="backward",
    )
    refs = jnp.concatenate([meta[2:3, 0:structs], far_meta[2:3, 0:structs], jnp.zeros((1, 128 - 2 * structs), F32)], axis=1)
    force_near, force_far, adj, pot = call(
        force_kernel,
        [((slots, atoms, width),)] * 2 + [((work, 128),), ((8, 128),)],
        (sums, sums_came, refs, meta, member, f),
        size=2 * 1024 * 1024,
        name="force",
    )
    force_came = to[4](force_far)
    tail = 8
    group = 4 * rows
    keep, give = call(
        gradient_kernel,
        [((2 * group + tail, hidden),)] * 2,
        (adj, pot, h1, h2, g2, g1, x),
        scratch=[pltpu.VMEM((width, hidden), F32), pltpu.VMEM((hidden, hidden), F32)],
        flops=6 * work * hidden * (width + hidden),
        size=4 * 1024 * 1024,
        name="gradient",
    )

    def halve(keep, came, end, name):
        left = (keep.shape[0] - end) // 2 + end
        return call(halving_kernel, [((left, hidden),)] * 2, (keep, came), size=4 * 4 * left * hidden, name=name)

    far_stay, far_leave, near_stay, near_leave = call(
        core_kernel,
        [((group // 2 + tail, hidden),)] * 2 + [((group // 2, hidden),)] * 2,
        (keep, to_core(give)),
        name="core_sum",
    )
    far_came = to[1](far_leave)
    far_stay, far_leave = halve(far_stay, far_came, tail, "far_x")
    near_came = to[1](near_leave)
    far_came = to[2](far_leave)
    near_stay, near_leave = halve(near_stay, near_came, 0, "near_x")
    token = force_came[0, 0:8, 0:128]
    token = to_core(token)
    (beyond_sum,) = call(sum_kernel, [((rows + tail, hidden),)], (far_stay, far_came, token), name="far_z")
    came = to[4](beyond_sum)
    last_came = to[2](near_leave)
    shape = lambda x: jax.ShapeDtypeStruct(x.shape, F32)
    vec_mom = vector_momentum.transpose(1, 0, 2)
    mine_first, mine_second, force_partials = pl.pallas_call(
        near_kernel,
        out_shape=[
            jax.ShapeDtypeStruct((1, first_layer.shape[1]), F32), jax.ShapeDtypeStruct((1, second_layer.shape[1]), F32),
            shape(descriptors),
        ],
        in_specs=[vmem] * 4,
        out_specs=[vmem] * 2 + [any_space],
        scratch_shapes=[pltpu.VMEM((rows, hidden), F32), pltpu.SemaphoreType.DMA((2,))],
        compiler_params=pltpu.CompilerParams(vmem_limit_bytes=8 * 1024 * 1024),
        cost_estimate=pl.CostEstimate(flops=1, bytes_accessed=1, transcendentals=0),
        name="near_z",
    )(near_stay, last_came, force_near, force_came)
    (
        new_first, new_second, new_vec, new_first_mom, new_second_mom, new_vec_mom, potential,
    ) = pl.pallas_call(
        final_kernel,
        out_shape=[
            shape(first_layer), shape(second_layer), shape(vec), shape(first_layer), shape(second_layer), shape(vec),
            jax.ShapeDtypeStruct((1, 128), F32),
        ],
        in_specs=[vmem] * 10,
        out_specs=[vmem] * 7,
        scratch_shapes=[pltpu.VMEM(first_layer.shape, F32), pltpu.VMEM(second_layer.shape, F32)],
        compiler_params=pltpu.CompilerParams(vmem_limit_bytes=8 * 1024 * 1024),
        cost_estimate=pl.CostEstimate(flops=1, bytes_accessed=1, transcendentals=0),
        name="final",
    )(
        mine_first, mine_second, beyond_sum, came, first_layer, second_layer, vec, first_momentum, second_momentum, vec_mom,
    )
    return (
        new_first, new_second, new_vec.transpose(1, 0, 2), new_first_mom, new_second_mom,
        new_vec_mom.transpose(1, 0, 2), potential[0, 0:1], force_partials,
    )


def element_energies(first, second, vectors, desc):
    lower = jnp.einsum("erf,efj->erj", desc, first, precision=HIGH) + vectors[:, 0][:, None, :]
    hidden = jnp.tanh(lower)
    upper = jnp.einsum("erj,ejk->erk", hidden, second, precision=HIGH) + vectors[:, 1][:, None, :]
    top = jnp.tanh(upper)
    return jnp.einsum("erk,ek->er", top, vectors[:, 2], precision=HIGH)


def structure_terms(energies, live, ids, refs):
    member = (
        ids[..., None] == jnp.arange(refs.shape[0], dtype=jnp.int32)[None, None, None, :]
    ).astype(jnp.float32)
    total = jnp.einsum("ebas,eba->s", member, energies, precision=HIGH)
    count = jnp.maximum(jnp.einsum("ebas,eba->s", member, live, precision=HIGH), 1.0)
    error = total / count - refs
    potential_part = jnp.sum(error * error) / (2.0 * NOISE_VAR)
    scale = error / count / NOISE_VAR
    adjoint = jnp.einsum("ebas,s->eba", member, scale, precision=HIGH) * live
    return (potential_part, adjoint)


def on_device(
    descriptors,
    counts,
    struct_ids,
    ref_energy,
    first_layer,
    second_layer,
    vectors,
    first_momentum,
    second_momentum,
    vector_momentum,
):
    nelem, slots, atoms, width = descriptors.shape
    hidden_width = vectors.shape[2]
    flat_first, flat_second = (
        lax.all_gather(first_layer, ("dp", "rep"), axis=1, tiled=True),
        lax.all_gather(second_layer, ("dp", "rep"), axis=1, tiled=True),
    )
    params = (
        flat_first.reshape(nelem, width, hidden_width),
        flat_second.reshape(nelem, hidden_width, hidden_width),
        vectors,
    )
    positions = jnp.arange(atoms, dtype=jnp.int32)
    live = (positions[None, None, :] < counts[:, :, None]).astype(jnp.float32)

    def forward(block):
        number = block.shape[1]

        def energy_fn(weights, pieces):
            flat = pieces.reshape(nelem, number * atoms, width)
            return element_energies(weights[0], weights[1], weights[2], flat).reshape(
                nelem, number, atoms
            )

        return jax.vjp(energy_fn, params, block)

    raw, pull = forward(descriptors)
    potential_part, adjoint = structure_terms(raw * live, live, struct_ids, ref_energy)
    grads, force_partials = pull(adjoint)
    grad_first = grads[0].reshape(nelem, width * hidden_width)
    grad_second = grads[1].reshape(nelem, hidden_width * hidden_width)
    sum_first, sum_second, grad_vectors, potential_sum = lax.psum(
        (grad_first, grad_second, grads[2], potential_part), ("dp", "rep")
    )
    position = lax.axis_index(("dp", "rep"))
    share_first = lax.dynamic_slice_in_dim(
        sum_first, position * first_layer.shape[1], first_layer.shape[1], 1
    )
    share_second = lax.dynamic_slice_in_dim(
        sum_second, position * second_layer.shape[1], second_layer.shape[1], 1
    )
    new_first_mom = first_momentum - STEP_SIZE * share_first
    new_second_mom = second_momentum - STEP_SIZE * share_second
    new_vector_mom = vector_momentum - STEP_SIZE * grad_vectors
    new_first = first_layer + STEP_SIZE * new_first_mom
    new_second = second_layer + STEP_SIZE * new_second_mom
    new_vectors = vectors + STEP_SIZE * new_vector_mom
    potential = (potential_sum / (ref_energy.shape[0] * lax.axis_size(("dp", "rep")))).reshape(1)
    return (
        new_first,
        new_second,
        new_vectors,
        new_first_mom,
        new_second_mom,
        new_vector_mom,
        potential,
        force_partials,
    )


def solution(mesh):
    placed = (
        P(None, ("dp", "rep"), None, None),
        P(None, ("dp", "rep")),
        P(None, ("dp", "rep"), None),
        P(("dp", "rep")),
        P("chain", ("dp", "rep")),
        P("chain", ("dp", "rep")),
        P("chain", None, None),
        P("chain", ("dp", "rep")),
        P("chain", ("dp", "rep")),
        P("chain", None, None),
    )
    split_by_half = (mesh.shape["chain"], mesh.shape["dp"], mesh.shape["rep"]) == (2, 8, 2)
    return jax.shard_map(
        halves if split_by_half else on_device,
        mesh=mesh,
        in_specs=placed,
        out_specs=(
            P("chain", ("dp", "rep")),
            P("chain", ("dp", "rep")),
            P("chain", None, None),
            P("chain", ("dp", "rep")),
            P("chain", ("dp", "rep")),
            P("chain", None, None),
            P("chain"),
            P("chain", ("dp", "rep"), None, None),
        ),
        check_vma=False,
    )
```
